32 devices in a mesh: batch: 2 (over core), seq: 16 (over z, y, x).
Axes of the slice: x: 2, y: 2, z: 4, core: 2. Of those that a mesh axis runs over, the one named last changes fastest.
Arguments:
- tokens: float32 [4, 4096, 768], P('batch', 'seq'), may hold values from -6 to 6
- cotangent: float32 [4, 4096, 768], P('batch', 'seq'), may hold values from -6 to 6
- prefix_len: int32 [4], P('batch'), may hold values from 409 to 4096, as said below
- query_routes: int32 [4, 512], P('batch'), may hold values from 0 to 4095, as said below
- key_routes: int32 [4, 512], P('batch'), may hold values from 0 to 4095, as said below
- ffn_routes: int32 [4, 512], P('batch'), may hold values from 0 to 4095, as said below
- light_qkv: bfloat16 [768, 1536], P(('batch', 'seq')), may hold values from -0.21875 to 0.21875
- light_out: bfloat16 [768, 512], P(('batch', 'seq')), may hold values from -1 to 1
- heavy_qkv: bfloat16 [768, 2304], P(('batch', 'seq')), may hold values from -0.21875 to 0.21875
- heavy_out: bfloat16 [768, 768], P(('batch', 'seq')), may hold values from -0.875 to 0.875
- light_ff_in: bfloat16 [768, 2048], P(('batch', 'seq')), may hold values from -0.21875 to 0.21875
- light_ff_out: bfloat16 [768, 1024], P(('batch', 'seq')), may hold values from -0.1875 to 0.1875
- heavy_ff_in: bfloat16 [768, 8192], P(('batch', 'seq')), may hold values from -0.21875 to 0.21875
- heavy_ff_out: bfloat16 [768, 4096], P(('batch', 'seq')), may hold values from -0.1875 to 0.1875
- gains: bfloat16 [768, 2], P(('batch', 'seq')), may hold values from 0.099609375 to 1.8984375
- routers: bfloat16 [768, 3], P(('batch', 'seq')), may hold values from -0.21875 to 0.21875
Outputs:
- output: float32 [4, 4096, 768], P('batch', 'seq')
- grad_tokens: float32 [4, 4096, 768], P('batch', 'seq')
- grad_light_qkv: float32 [768, 1536], P(('batch', 'seq'))
- grad_light_out: float32 [768, 512], P(('batch', 'seq'))
- grad_heavy_qkv: float32 [768, 2304], P(('batch', 'seq'))
- grad_heavy_out: float32 [768, 768], P(('batch', 'seq'))
- grad_light_ff_in: float32 [768, 2048], P(('batch', 'seq'))
- grad_light_ff_out: float32 [768, 1024], P(('batch', 'seq'))
- grad_heavy_ff_in: float32 [768, 8192], P(('batch', 'seq'))
- grad_heavy_ff_out: float32 [768, 4096], P(('batch', 'seq'))
- grad_gains: float32 [768, 2], P(('batch', 'seq'))
- grad_routers: float32 [768, 3], P(('batch', 'seq'))
The draws below stay inside these ranges and needn't reach their ends.
Inputs may be any that keep to these rules, and one draw needn't show every extreme that they name: `prefix_len`: in each aligned group of 2 sequences, one sequence has a prefix of 3904 tokens or more; all others have a prefix of 409 to 2048 tokens. `query_routes`: each row lists 512 distinct token positions of its sequence in increasing order, the first being 0 and the last 4095. At most 64 of them lie among the 256 positions of one device along seq, and in every row some device holds exactly 64. `key_routes`: each row lists 512 distinct token positions of its sequence in increasing order, the first being 0 and the last 4095. At most 64 of them lie among the 256 positions of one device along seq, and in every row some device holds exactly 64. `ffn_routes`: each row lists 512 distinct token positions of its sequence in increasing order, the first being 0 and the last 4095. At most 64 of them lie among the 256 positions of one device along seq, and in every row some device holds exactly 64.
All inputs are finite; a program needn't handle non-finite values.
Results may differ from the reference program's by a relative error of at most 0.0003.
Values may be sent and summed in bfloat16 or wider, within the bound.
No kernel may reach another device: no remote copies, remote signals or barrier semaphores. Data moves between devices by JAX's collectives and lax.ppermute only.
A program may use at most 320 MiB of HBM per device.

```python
import jax
import jax.numpy as jnp
from jax import lax

D = 768
HL = 8
HH = 12
DH = 64
FL = 1024
FH = 4096
W = 128
TOK_DEV = 256
SEQS = 2
IL = 512
IH = 768
LENGTH = 4096
BATCH = 4
ROUTED = 512


def block_permutation(sub_key):
    return jax.random.permutation(sub_key, TOK_DEV).astype(jnp.int32)


def route_row(row_key):
    blocks = LENGTH // TOK_DEV
    mean_count = TOK_DEV // 8
    key_order, key_shift, key_rank = jax.random.split(row_key, 3)
    block_order = jax.random.permutation(key_order, blocks).astype(jnp.int32)
    counts = jnp.full((blocks,), mean_count, jnp.int32)
    counts = counts.at[block_order[0]].add(mean_count)
    counts = counts.at[block_order[1]].add(-(mean_count // 2))
    counts = counts.at[block_order[2]].add(-(mean_count // 2))
    pair_count = (blocks - 3) // 2
    shifts = jax.random.randint(key_shift, (pair_count,), 0, mean_count, dtype=jnp.int32)
    counts = counts.at[block_order[3:3 + 2 * pair_count:2]].add(shifts)
    counts = counts.at[block_order[4:4 + 2 * pair_count:2]].add(-shifts)
    rank_table = jax.vmap(block_permutation)(jax.random.split(key_rank, blocks))
    first_rank = rank_table[0, 0]
    head_row = jnp.where(rank_table[0] == 0, first_rank, rank_table[0]).at[0].set(0)
    rank_table = rank_table.at[0].set(head_row)
    last_rank = rank_table[blocks - 1, TOK_DEV - 1]
    tail_row = jnp.where(rank_table[blocks - 1] == 0, last_rank, rank_table[blocks - 1]).at[TOK_DEV - 1].set(0)
    rank_table = rank_table.at[blocks - 1].set(tail_row)
    chosen = (rank_table < counts[:, None]).reshape(-1)
    return jnp.nonzero(chosen, size=ROUTED)[0].astype(jnp.int32)


def route_table(base_key, salt):
    return jax.vmap(route_row)(jax.random.split(jax.random.fold_in(base_key, salt), BATCH))


def draw_query_routes(key, part):
    return route_table(key, 11)


def draw_key_routes(key, part):
    return route_table(key, 12)


def draw_ffn_routes(key, part):
    return route_table(key, 13)


def draw_prefix_len(key, part):
    key_short, key_long, key_pick = jax.random.split(jax.random.fold_in(key, 21), 3)
    short_len = jax.random.randint(key_short, (BATCH,), LENGTH // 10, LENGTH // 2 + 1, dtype=jnp.int32)
    long_len = jax.random.randint(key_long, (BATCH,), LENGTH - TOK_DEV + W // 2, LENGTH + 1, dtype=jnp.int32)
    picked = jax.random.randint(key_pick, (BATCH // SEQS,), 0, SEQS, dtype=jnp.int32)
    picked_rows = jnp.repeat(picked, SEQS, total_repeat_length=BATCH)
    within_group = jnp.arange(BATCH, dtype=jnp.int32) % SEQS
    return jnp.where(within_group == picked_rows, long_len, short_len).astype(jnp.int32)


def strengthened(result, key, source, target, parts, factor):
    def block_of(position):
        return (jnp.arange(result.shape[position]) // (result.shape[position] // parts)).reshape((-1,) + (1,) * (result.ndim - 1 - position))

    first = jax.random.permutation(key, parts)[block_of(target)]
    far = (block_of(target) + parts // 2) % parts
    return jnp.where((block_of(source) == first) | (block_of(source) == far), factor * result, result)


def shard_levels(rng, dims, shards, smallest, top_value):
    def one(dim, shards_of):
        heights = jax.random.uniform(jax.random.fold_in(jax.random.fold_in(rng, 6), dim), (shards_of,), jnp.float32, smallest / len(shards), top_value / len(shards))
        return jnp.repeat(jnp.exp(heights), dims[dim] // shards_of).reshape((-1,) + (1,) * (len(dims) - dim - 1))

    level = one(*shards[0])
    for cut in shards[1:]:
        level = level * one(*cut)
    return level


def bell_draw(key, shape, width, most, cuts=(), held_as=jnp.bfloat16):
    result = jax.random.normal(key, shape, jnp.float32) * width
    if len(cuts) > 0:
        result = shard_levels(key, shape, cuts, -0.22, 0.18) * result
    return jnp.clip(result, min=-most, max=most).astype(held_as)


def gaussian_with(own_key, dims, spread, most, cuts, heavy, kind=jnp.bfloat16):
    result = spread * jax.random.normal(own_key, dims, jnp.float32)
    if cuts:
        result = result * shard_levels(own_key, dims, cuts, -0.22, 0.18)
    return jnp.clip(strengthened(result, jax.random.fold_in(own_key, 3), *heavy), -most, most).astype(kind)


def setup_inputs(seed: int = 0) -> dict:
    key_of = jax.random.split(jax.random.key(seed), 17)
    tokens = bell_draw(key_of[0], (BATCH, LENGTH, D), 1.0, 6.0, ((0, 2), (1, 16)), jnp.float32)
    cotangent = gaussian_with(key_of[1], (BATCH, LENGTH, D), 1.0, 6.0, ((0, 2), (1, 16)), (1, 2, 16, 2.0), jnp.float32)
    prefix_len = draw_prefix_len(jax.random.fold_in(key_of[16], 71), 0)
    query_routes = draw_query_routes(jax.random.fold_in(key_of[16], 71), 0)
    key_routes = draw_key_routes(jax.random.fold_in(key_of[16], 71), 0)
    ffn_routes = draw_ffn_routes(jax.random.fold_in(key_of[16], 71), 0)
    light_qkv = bell_draw(key_of[6], (D, 3 * IL), D ** -0.5, 0.21875, ((0, 32),))
    light_out = bell_draw(key_of[7], (D, IL), (IL // 16) ** -0.5, 1.0, ((0, 32),))
    heavy_qkv = bell_draw(key_of[8], (D, 3 * IH), D ** -0.5, 0.21875, ((0, 32),))
    heavy_out = bell_draw(key_of[9], (D, IH), (IH // 16) ** -0.5, 0.875, ((0, 32),))
    light_ff_in = bell_draw(key_of[10], (D, 2 * FL), D ** -0.5, 0.21875, ((0, 32),))
    light_ff_out = bell_draw(key_of[11], (D, FL), FL ** -0.5, 0.1875, ((0, 32),))
    heavy_ff_in = bell_draw(key_of[12], (D, 2 * FH), D ** -0.5, 0.21875, ((0, 32),))
    heavy_ff_out = bell_draw(key_of[13], (D, FH), (FH // 4) ** -0.5, 0.1875, ((0, 32),))
    gains = jnp.clip(1.0 + 0.18 * jax.random.normal(key_of[14], (D, 2), jnp.float32), 0.099609375, 1.8984375).astype(jnp.bfloat16)
    routers = bell_draw(key_of[15], (D, 3), D ** -0.5, 0.21875, ((0, 32),))
    return dict(tokens=tokens, cotangent=cotangent, prefix_len=prefix_len, query_routes=query_routes, key_routes=key_routes, ffn_routes=ffn_routes, light_qkv=light_qkv, light_out=light_out, heavy_qkv=heavy_qkv, heavy_out=heavy_out, light_ff_in=light_ff_in, light_ff_out=light_ff_out, heavy_ff_in=heavy_ff_in, heavy_ff_out=heavy_ff_out, gains=gains, routers=routers)


precise_mode = lax.Precision.HIGHEST
eps = 1e-06

@jax.custom_vjp
def low(v):
    return lax.optimization_barrier(v.astype(jnp.bfloat16)).astype(jnp.float32)

@jax.custom_vjp
def low_back(v):
    return v

def low_keep(v):
    return (low(v), None)

def low_pass(kept, grad):
    return (grad,)

def back_keep(v):
    return (v, None)

def back_low(kept, grad):
    return (low(grad),)
low.defvjp(low_keep, low_pass)
low_back.defvjp(back_keep, back_low)

def rms_scale(values, gain_vec):
    return values * lax.rsqrt(lax.optimization_barrier(jnp.mean(values * values, axis=-1, keepdims=True)) + eps) * gain_vec

def gelu_tanh(values):
    return jax.nn.gelu(values, approximate=True)

def matmul(left_side, right_side):
    return jnp.dot(left_side, right_side, precision=precise_mode, preferred_element_type=jnp.float32)

def masked_softmax(scores, allowed):
    return jax.nn.softmax(jnp.where(allowed, scores, -1e+30), axis=-1)

def light_attention(queries, key_mat, value_mat, prefix):
    block_rows = min(512, LENGTH)
    block_count = LENGTH // block_rows
    zero_rim = jnp.zeros((W, IL), jnp.float32)
    key_pad = jnp.concatenate([zero_rim, key_mat, zero_rim], axis=0)
    value_pad = jnp.concatenate([zero_rim, value_mat, zero_rim], axis=0)

    @jax.checkpoint
    def one_block(start_row):
        span_rows = block_rows + 2 * W
        query_heads = lax.dynamic_slice_in_dim(queries, start_row, block_rows, 0).reshape(block_rows, HL, DH)
        key_heads = lax.dynamic_slice_in_dim(key_pad, start_row, span_rows, 0).reshape(span_rows, HL, DH)
        value_heads = lax.dynamic_slice_in_dim(value_pad, start_row, span_rows, 0).reshape(span_rows, HL, DH)
        query_pos = start_row + jnp.arange(block_rows, dtype=jnp.int32)
        key_pos = start_row - W + jnp.arange(span_rows, dtype=jnp.int32)
        within_window = jnp.abs(query_pos[:, None] - key_pos[None, :]) < W
        inside = (key_pos >= 0) & (key_pos < LENGTH)
        causal = (key_pos[None, :] <= query_pos[:, None]) | (key_pos[None, :] < prefix)
        allowed = within_window & inside[None, :] & causal
        scores = jnp.einsum('thd,uhd->htu', query_heads, key_heads, precision=precise_mode) * DH ** (-0.5)
        attn_probs = masked_softmax(scores, allowed[None])
        mixed_heads = jnp.einsum('htu,uhd->thd', attn_probs, value_heads, precision=precise_mode)
        return mixed_heads.reshape(block_rows, IL)
    starts = jnp.arange(block_count, dtype=jnp.int32) * block_rows
    return lax.map(one_block, starts).reshape(LENGTH, IL)

@jax.checkpoint
def heavy_attention(queries, key_mat, value_mat, query_pos, key_pos, prefix):
    query_heads = queries.reshape(-1, HH, DH)
    key_heads = key_mat.reshape(-1, HH, DH)
    value_heads = value_mat.reshape(-1, HH, DH)
    allowed = (key_pos[None, :] <= query_pos[:, None]) | (key_pos[None, :] < prefix)
    scores = jnp.einsum('qhd,khd->hqk', query_heads, key_heads, precision=precise_mode) * DH ** (-0.5)
    attn_probs = masked_softmax(scores, allowed[None])
    mixed_heads = jnp.einsum('hqk,khd->qhd', attn_probs, value_heads, precision=precise_mode)
    return mixed_heads.reshape(-1, IH)

def layer_forward(tokens_one, prefix, q_routes, k_routes, f_routes, weight_set):
    light_qkv, light_out, heavy_qkv, heavy_out, light_ff_in, light_ff_out, heavy_ff_in, heavy_ff_out, gains, routers = weight_set
    normed = rms_scale(tokens_one, gains[:, 0])
    light_proj = matmul(normed, light_qkv)
    attended = light_attention(light_proj[:, :IL], light_proj[:, IL:2 * IL], light_proj[:, 2 * IL:], prefix)
    light_branch = matmul(attended, light_out.T)
    query_rows = jnp.take(normed, q_routes, axis=0)
    key_rows = jnp.take(normed, k_routes, axis=0)
    query_score = jax.nn.sigmoid(matmul(query_rows, routers[:, 0]))
    key_score = jax.nn.sigmoid(matmul(key_rows, routers[:, 1]))
    heavy_query = matmul(query_rows, heavy_qkv[:, :IH])
    heavy_key = matmul(key_rows, heavy_qkv[:, IH:2 * IH])
    heavy_value = matmul(key_rows, heavy_qkv[:, 2 * IH:]) * key_score[:, None]
    heavy_mixed = heavy_attention(heavy_query, heavy_key, heavy_value, q_routes, k_routes, prefix)
    heavy_rows = matmul(heavy_mixed, heavy_out.T) * query_score[:, None]
    hidden = tokens_one + light_branch + jnp.zeros_like(tokens_one).at[q_routes].add(heavy_rows)
    second = rms_scale(hidden, gains[:, 1])
    gate_up = matmul(second, light_ff_in)
    light_ff = matmul(gelu_tanh(gate_up[:, :FL]) * gate_up[:, FL:], light_ff_out.T)
    ffn_rows = jnp.take(second, f_routes, axis=0)
    ffn_score = jax.nn.sigmoid(matmul(ffn_rows, routers[:, 2]))
    heavy_gate_up = matmul(ffn_rows, heavy_ff_in)
    heavy_ff = matmul(gelu_tanh(heavy_gate_up[:, :FH]) * heavy_gate_up[:, FH:], heavy_ff_out.T) * ffn_score[:, None]
    return hidden + light_ff + jnp.zeros_like(tokens_one).at[f_routes].add(heavy_ff)

def reference(tokens, cotangent, prefix_len, query_routes, key_routes, ffn_routes, light_qkv, light_out, heavy_qkv, heavy_out, light_ff_in, light_ff_out, heavy_ff_in, heavy_ff_out, gains, routers):
    weight_set = tuple((piece.astype(jnp.float32) for piece in (light_qkv, light_out, heavy_qkv, heavy_out, light_ff_in, light_ff_out, heavy_ff_in, heavy_ff_out, gains, routers)))

    def forward(tokens_all, weights_in):

        def scan_step(carry_in, item_in):
            tokens_one, prefix, q_routes, k_routes, f_routes = item_in
            return (carry_in, layer_forward(tokens_one, prefix, q_routes, k_routes, f_routes, weights_in))
        _, outputs = lax.scan(scan_step, jnp.zeros((), jnp.float32), (tokens_all, prefix_len, query_routes, key_routes, ffn_routes))
        return outputs
    output, pullback = jax.vjp(forward, tokens, weight_set)
    grad_tokens, grad_weights = pullback(cotangent)
    return (output, grad_tokens, grad_weights[0], grad_weights[1], grad_weights[2], grad_weights[3], grad_weights[4], grad_weights[5], grad_weights[6], grad_weights[7], grad_weights[8], grad_weights[9])
```

```python
import jax
import jax.numpy as jnp
from jax import lax
from jax.sharding import PartitionSpec as P

HL = 8
HH = 12
DH = 64
FL = 1024
FH = 4096
W = 128
IL = 512
IH = 768
GROUP = 4

f32 = jnp.float32
bf16 = jnp.bfloat16
fine = lax.Precision.HIGH
eps = 1e-06
GELU_A = 0.7978845608
GELU_B = 0.044715


def bit_stages(axis):
    size, found, step = lax.axis_size(axis), [], 1
    while step < size:
        found.append((axis, step))
        step *= 2
    return found


def own_bit(stage):
    axis, step = stage
    return (lax.axis_index(axis) // step) % 2


def flip(value, axis, step):
    return lax.ppermute(value, axis, [(i, i ^ step) for i in range(lax.axis_size(axis))])


def swapped(order):
    order = list(order)
    order[0], order[1] = order[1], order[0]
    return order


def gather_blocks(value, order, canonical):
    shape, have = value.shape, []
    for stage in order:
        other = flip(value, *stage)
        mine = own_bit(stage) == 1
        at = sum(1 for s in have if canonical.index(s) < canonical.index(stage))
        low = jnp.where(mine, other, value)
        high = jnp.where(mine, value, other)
        value = jnp.stack([low, high], axis=at)
        have = sorted(have + [stage], key=canonical.index)
    return value.reshape((2 ** len(order),) + shape)


def scatter_blocks(value, order, canonical):
    have = [s for s in canonical if s in order]
    shape = value.shape[1:]
    value = value.reshape((2,) * len(have) + shape)
    for stage in order:
        at, mine = have.index(stage), own_bit(stage)
        sent = lax.dynamic_index_in_dim(value, 1 - mine, at, keepdims=False)
        kept = lax.dynamic_index_in_dim(value, mine, at, keepdims=False)
        value = kept + flip(sent, *stage)
        have.remove(stage)
    return value


def in_group_order(pieces):
    value = jnp.stack(pieces)
    value = value.reshape((2, 2) + value.shape[1:])
    place = lax.axis_index("seq") % GROUP
    value = jnp.where(place // 2 == 1, value[::-1], value)
    value = jnp.where(place % 2 == 1, value[:, ::-1], value)
    return value.reshape((GROUP,) + value.shape[2:])


def shifted(value, by):
    length = lax.axis_size("seq")
    pairs = [(i, i + by) for i in range(length) if 0 <= i + by < length]
    return lax.ppermute(value, "seq", pairs)


def product(formula, left_side, right_side):
    return jnp.einsum(
        formula,
        left_side.astype(f32),
        right_side.astype(f32),
        precision=fine,
        preferred_element_type=f32,
    )


def unit_rms(values):
    scale = lax.rsqrt(jnp.mean(values * values, axis=-1, keepdims=True) + eps)
    return values * scale, scale


def norm_back(unit, scale, scaled_grad):
    return scale * (scaled_grad - unit * jnp.mean(scaled_grad * unit, axis=-1, keepdims=True))


def gelu_both(values):
    squared = values * values
    bend = jnp.tanh(GELU_A * (values + GELU_B * squared * values))
    half = 0.5 * (1.0 + bend)
    slope = half + 0.5 * values * (1.0 - bend * bend) * GELU_A * (1.0 + 3.0 * GELU_B * squared)
    return values * half, slope


def local_slots(route_row, row_begin, span_rows, capacity):
    below = jnp.sum((route_row < row_begin).astype(jnp.int32))
    upper = jnp.sum((route_row < row_begin + span_rows).astype(jnp.int32))
    slot = below + jnp.arange(capacity, dtype=jnp.int32)
    index = jnp.arange(route_row.shape[0], dtype=jnp.int32)
    positions = jnp.sum(
        jnp.where(slot[:, None] == index[None, :], route_row[None, :], 0), axis=1
    )
    offsets = positions - row_begin
    matched = (offsets[:, None] == jnp.arange(span_rows, dtype=jnp.int32)[None, :]) & (
        slot < upper
    )[:, None]
    return positions, matched.astype(bf16)


def slot_table(route_row, span_rows, devices, capacity):
    home = route_row // span_rows
    before = jnp.sum((route_row[None, :] < (home * span_rows)[:, None]).astype(jnp.int32), axis=1)
    rank = jnp.arange(route_row.shape[0], dtype=jnp.int32) - before
    place = home * capacity + rank
    return (
        place[:, None] == jnp.arange(devices * capacity, dtype=jnp.int32)[None, :]
    ).astype(bf16)


def softmax(scores, allowed):
    scores = jnp.where(allowed, scores, -1e30)
    top = jnp.max(scores, axis=-1, keepdims=True)
    weights = jnp.exp(scores - top)
    return weights / jnp.sum(weights, axis=-1, keepdims=True)


def light_blocks(kv_ext, rows):
    seqs = kv_ext.shape[0]
    parts = kv_ext.reshape(seqs, rows // W + 2, W, 2, HL, DH)
    spans = jnp.stack([parts[:, b : b + 3] for b in range(rows // W)], axis=1)
    spans = spans.reshape(seqs, rows // W, 3 * W, 2, HL, DH)
    return spans[:, :, :, 0], spans[:, :, :, 1]


def on_device(
    tokens,
    cotangent,
    prefix_len,
    query_routes,
    key_routes,
    ffn_routes,
    light_qkv,
    light_out,
    heavy_qkv,
    heavy_out,
    light_ff_in,
    light_ff_out,
    heavy_ff_in,
    heavy_ff_out,
    gains,
    routers,
):
    seqs, rows, width = tokens.shape
    devices = lax.axis_size("seq")
    row_begin = lax.axis_index("seq") * rows
    full_len = rows * devices
    capacity = rows // 4
    place = lax.axis_index("seq") % GROUP
    units = FH // GROUP

    seq_bits = bit_stages("seq")
    batch_bits = bit_stages("batch")
    canonical = batch_bits[::-1] + seq_bits[::-1]
    down_a = batch_bits + seq_bits
    down_b = batch_bits + swapped(seq_bits)
    up_a = down_a[::-1]
    up_b = down_b[::-1]
    seq_canonical = seq_bits[::-1]
    seq_down = (seq_bits, swapped(seq_bits))
    group_bits = seq_bits[:2]
    far_bits = seq_bits[2:]

    def joined(*pieces):
        return jnp.concatenate(pieces, axis=1)

    def gather_weight(value, order):
        return gather_blocks(value, order, canonical).reshape(-1, value.shape[1])

    def scatter_weight(value, order):
        blocks = 2 ** len(canonical)
        return scatter_blocks(
            value.reshape(blocks, value.shape[0] // blocks, value.shape[1]), order, canonical
        )

    def group_gather(value):
        canon = group_bits[::-1]
        first = gather_blocks(value[0], canon, canon)
        second_ = gather_blocks(value[1], group_bits, canon)
        return jnp.stack([first, second_], axis=1)

    n_one, r_one = unit_rms(tokens)
    small = gather_weight(joined(gains, routers), up_a).astype(f32)
    gain_one, gain_two = small[:, 0], small[:, 1]
    router_q, router_k, router_f = small[:, 2], small[:, 3], small[:, 4]
    before = shifted(tokens[:, rows - W :], 1)
    after = shifted(tokens[:, :W], -1)

    def picker(route_row):
        return local_slots(route_row, row_begin, rows, capacity)

    query_at, query_pick = jax.vmap(picker)(query_routes)
    _, key_pick = jax.vmap(picker)(key_routes)
    _, ffn_pick = jax.vmap(picker)(ffn_routes)
    table = jax.vmap(lambda r: slot_table(r, rows, devices, capacity))(key_routes)

    picked = product("sct,std->scd", jnp.concatenate([query_pick, key_pick], axis=1), n_one)
    query_unit, key_unit_own = picked[:, :capacity], picked[:, capacity:]

    qkv_light = gather_weight(light_qkv, up_a)
    qkv_heavy = gather_weight(heavy_qkv, up_b)
    key_slots = jnp.stack(
        [
            gather_blocks(key_unit_own[s], seq_down[s % 2][::-1], seq_canonical).reshape(-1, width)
            for s in range(seqs)
        ]
    )
    outs = gather_weight(joined(light_out, heavy_out), up_a)
    out_light, out_heavy = outs[:, :IL], outs[:, IL:]
    ff_in = gather_weight(light_ff_in, up_b)
    ff_out = gather_weight(light_ff_out, up_a)

    def unit_slice(gate_up, down, who):
        return joined(
            lax.dynamic_slice_in_dim(gate_up, who * units, units, 1),
            lax.dynamic_slice_in_dim(gate_up, FH + who * units, units, 1),
            lax.dynamic_slice_in_dim(down, who * units, units, 1),
        )

    big = in_group_order(
        [unit_slice(heavy_ff_in, heavy_ff_out, place)]
        + [
            flip(unit_slice(heavy_ff_in, heavy_ff_out, place ^ j), "seq", j)
            for j in range(1, GROUP)
        ]
    )
    big = gather_blocks(big, (batch_bits + far_bits)[::-1], batch_bits[::-1] + far_bits[::-1])
    big = big.reshape(width, 3 * units)
    big_in, big_out = big[:, : 2 * units], big[:, 2 * units :]

    cot_rows = group_gather(product("sct,std->scd", ffn_pick, cotangent))
    cot_rows = cot_rows.reshape(-1, width)

    n_ext = unit_rms(jnp.concatenate([before, tokens, after], axis=1))[0]
    normed_ext = n_ext * gain_one
    normed = n_one * gain_one
    light_q = product("std,de->ste", normed, qkv_light[:, :IL])
    light_kv = product("std,de->ste", normed_ext, qkv_light[:, IL:])
    blocks = rows // W
    q_heads = light_q.reshape(seqs, blocks, W, HL, DH)
    k_heads, v_heads = light_blocks(light_kv, rows)
    query_pos = (row_begin + jnp.arange(rows, dtype=jnp.int32)).reshape(blocks, W)
    key_pos = (
        row_begin
        - W
        + W * jnp.arange(blocks, dtype=jnp.int32)[:, None]
        + jnp.arange(3 * W, dtype=jnp.int32)[None, :]
    )
    near = jnp.abs(query_pos[:, :, None] - key_pos[:, None, :]) < W
    inside = (key_pos >= 0) & (key_pos < full_len)
    causal = (key_pos[None, :, None, :] <= query_pos[None, :, :, None]) | (
        key_pos[None, :, None, :] < prefix_len[:, None, None, None]
    )
    allowed = causal & near[None] & inside[None, :, None, :]
    scale = DH**-0.5
    light_probs = softmax(
        product("sbthd,sbuhd->sbhtu", q_heads, k_heads) * scale, allowed[:, :, None]
    )
    attended = product("sbhtu,sbuhd->sbthd", light_probs, v_heads).reshape(seqs, rows, IL)
    light_branch = product("sti,di->std", attended, out_light)

    query_rows = query_unit * gain_one
    key_unit = product("skp,spd->skd", table, key_slots)
    key_rows = key_unit * gain_one
    query_score = jax.nn.sigmoid(jnp.sum(query_rows * router_q, axis=-1))
    key_score = jax.nn.sigmoid(jnp.sum(key_rows * router_k, axis=-1))
    heavy_q = product("scd,di->sci", query_rows, qkv_heavy[:, :IH])
    heavy_kv = product("skd,de->ske", key_rows, qkv_heavy[:, IH:])
    heavy_k, heavy_v_raw = heavy_kv[..., :IH], heavy_kv[..., IH:]
    heavy_v = heavy_v_raw * key_score[..., None]
    hq = heavy_q.reshape(seqs, capacity, HH, DH)
    hk = heavy_k.reshape(seqs, -1, HH, DH)
    hv = heavy_v.reshape(seqs, -1, HH, DH)
    heavy_allowed = (key_routes[:, None, :] <= query_at[:, :, None]) | (
        key_routes[:, None, :] < prefix_len[:, None, None]
    )
    heavy_probs = softmax(product("schd,skhd->shck", hq, hk) * scale, heavy_allowed[:, None])
    heavy_mixed = product("shck,skhd->schd", heavy_probs, hv).reshape(seqs, capacity, IH)
    heavy_plain = product("sci,di->scd", heavy_mixed, out_heavy)
    heavy_rows = heavy_plain * query_score[..., None]
    hidden = tokens + light_branch + product("sct,scd->std", query_pick, heavy_rows)

    n_two, r_two = unit_rms(hidden)
    second = n_two * gain_two
    ffn_rows = group_gather(product("sct,std->scd", ffn_pick, second)).reshape(-1, width)
    gate_up = product("std,de->ste", second, ff_in)
    gate, up = gate_up[..., :FL], gate_up[..., FL:]
    gate_act, gate_slope = gelu_both(gate)
    light_act = gate_act * up
    light_ff = product("stf,df->std", light_act, ff_out)
    d_act = product("std,df->stf", cotangent, ff_out)
    d_gate_up = jnp.concatenate([d_act * up * gate_slope, d_act * gate_act], axis=-1)
    d_second = product("ste,de->std", d_gate_up, ff_in)
    d_ff_in = scatter_weight(product("std,ste->de", second, d_gate_up), down_b)
    d_ff_out = scatter_weight(product("std,stf->df", cotangent, light_act), down_a)

    ffn_score = jax.nn.sigmoid(jnp.sum(ffn_rows * router_f, axis=-1, keepdims=True))
    big_gate_up = product("rd,de->re", ffn_rows, big_in)
    big_gate, big_up = big_gate_up[:, :units], big_gate_up[:, units:]
    big_act, big_slope = gelu_both(big_gate)
    big_mix = big_act * big_up
    big_rows = product("rf,df->rd", big_mix, big_out) * ffn_score
    cot_mix = product("rd,df->rf", cot_rows, big_out)
    d_score = jnp.sum(cot_mix * big_mix, axis=-1, keepdims=True)
    d_score_in = d_score * ffn_score * (1.0 - ffn_score)
    d_mix = cot_mix * ffn_score
    d_big = jnp.concatenate([d_mix * big_up * big_slope, d_mix * big_act], axis=-1)
    d_ffn_rows = product("re,de->rd", d_big, big_in) + d_score_in * router_f
    d_router_f = jnp.sum(d_score_in * ffn_rows, axis=0)

    def group_blocks(value):
        return value.reshape(GROUP, seqs, capacity, width)

    ffn_own = scatter_blocks(group_blocks(d_ffn_rows), group_bits, group_bits[::-1])
    out_own = scatter_blocks(group_blocks(big_rows), swapped(group_bits), group_bits[::-1])
    d_big_all = joined(
        product("rd,re->de", ffn_rows, d_big),
        product("rd,rf->df", cot_rows, big_mix * ffn_score),
    )
    far_order = batch_bits + far_bits
    d_big_all = scatter_blocks(
        d_big_all.reshape(
            2 ** len(far_order), GROUP, width // 2 ** len(far_order) // GROUP, 3 * units
        ),
        far_order,
        batch_bits[::-1] + far_bits[::-1],
    )
    mine = in_group_order(
        [lax.dynamic_index_in_dim(d_big_all, place, 0, keepdims=False)]
        + [
            flip(lax.dynamic_index_in_dim(d_big_all, place ^ j, 0, keepdims=False), "seq", j)
            for j in range(1, GROUP)
        ]
    )

    def spread(value):
        return jnp.swapaxes(value, 0, 1).reshape(value.shape[1], -1)

    d_heavy_ff_in = joined(spread(mine[..., :units]), spread(mine[..., units : 2 * units]))
    d_heavy_ff_out = spread(mine[..., 2 * units :])

    output = hidden + light_ff + product("sct,scd->std", ffn_pick, out_own)
    d_second = d_second + product("sct,scd->std", ffn_pick, ffn_own)
    d_gain_two = jnp.sum(d_second * n_two, axis=(0, 1))
    d_hidden = cotangent + norm_back(n_two, r_two, d_second * gain_two)

    d_heavy_rows = product("sct,std->scd", query_pick, d_hidden)
    d_query_score = jnp.sum(d_heavy_rows * heavy_plain, axis=-1)
    d_plain = d_heavy_rows * query_score[..., None]
    d_mixed = product("scd,di->sci", d_plain, out_heavy)
    d_attended = product("std,di->sti", d_hidden, out_light)
    d_outs = scatter_weight(
        joined(
            product("std,sti->di", d_hidden, attended),
            product("scd,sci->di", d_plain, heavy_mixed),
        ),
        down_a,
    )
    d_mixed_heads = d_mixed.reshape(seqs, capacity, HH, DH)
    row_dot = jnp.sum(d_mixed_heads * heavy_mixed.reshape(d_mixed_heads.shape), axis=-1)
    d_probs = product("schd,skhd->shck", d_mixed_heads, hv)
    d_scores = heavy_probs * (d_probs - jnp.swapaxes(row_dot, 1, 2)[..., None]) * scale
    d_hv = product("shck,schd->skhd", heavy_probs, d_mixed_heads).reshape(heavy_v.shape)
    d_hq = product("shck,skhd->schd", d_scores, hk).reshape(heavy_q.shape)
    d_hk = product("shck,schd->skhd", d_scores, hq).reshape(heavy_k.shape)
    d_key_score = jnp.sum(d_hv * heavy_v_raw, axis=-1)
    d_key_in = d_key_score * key_score * (1.0 - key_score)
    d_query_in = d_query_score * query_score * (1.0 - query_score)
    d_kv = jnp.concatenate([d_hk, d_hv * key_score[..., None]], axis=-1)
    d_key_rows = product("ske,de->skd", d_kv, qkv_heavy[:, IH:]) + d_key_in[..., None] * router_k
    d_query_rows = (
        product("sci,di->scd", d_hq, qkv_heavy[:, :IH]) + d_query_in[..., None] * router_q
    )
    d_router_k = jnp.sum(d_key_in[..., None] * key_rows, axis=(0, 1))
    d_router_q = jnp.sum(d_query_in[..., None] * query_rows, axis=(0, 1))
    d_key_slots = product("skp,skd->spd", table, d_key_rows)
    d_key_own = jnp.stack(
        [
            scatter_blocks(
                d_key_slots[s].reshape(devices, capacity, width), seq_down[s % 2], seq_canonical
            )
            for s in range(seqs)
        ]
    )
    d_heavy_q_w = product("scd,sci->di", query_rows, d_hq)
    d_heavy_kv_w = product("skd,ske->de", key_rows, d_kv)
    d_qkv_heavy = scatter_weight(joined(d_heavy_q_w, d_heavy_kv_w), down_b)

    d_att_heads = d_attended.reshape(seqs, blocks, W, HL, DH)
    light_dot = jnp.sum(d_att_heads * attended.reshape(d_att_heads.shape), axis=-1)
    dl_probs = product("sbthd,sbuhd->sbhtu", d_att_heads, v_heads)
    dl_scores = light_probs * (dl_probs - jnp.swapaxes(light_dot, 2, 3)[..., None]) * scale
    d_lv = product("sbhtu,sbthd->sbuhd", light_probs, d_att_heads)
    d_lq = product("sbhtu,sbuhd->sbthd", dl_scores, k_heads).reshape(seqs, rows, IL)
    d_lk = product("sbhtu,sbthd->sbuhd", dl_scores, q_heads)

    def overlapped(value):
        value = value.reshape(seqs, blocks, 3, W, IL)
        total = jnp.zeros((seqs, blocks + 2, W, IL), f32)
        for b in range(blocks):
            total = total.at[:, b : b + 3].add(value[:, b])
        return total.reshape(seqs, rows + 2 * W, IL)

    d_lkv = jnp.concatenate([overlapped(d_lk), overlapped(d_lv)], axis=-1)
    d_ext = product("ste,de->std", d_lkv, qkv_light[:, IL:])
    from_next = shifted(d_ext[:, :W], -1)
    from_prev = shifted(d_ext[:, W + rows :], 1)
    d_qkv_light = scatter_weight(
        joined(product("std,ste->de", normed, d_lq), product("std,ste->de", normed_ext, d_lkv)),
        down_a,
    )
    d_own = product("ste,de->std", d_lq, qkv_light[:, :IL]) + product(
        "sct,scd->std", query_pick, d_query_rows
    )
    d_gain_one = (
        jnp.sum(d_ext * n_ext, axis=(0, 1))
        + jnp.sum(d_own * n_one, axis=(0, 1))
        + jnp.sum(d_key_rows * key_unit, axis=(0, 1))
    )
    d_normed = d_own + d_ext[:, W : W + rows] + product("sct,scd->std", key_pick, d_key_own)
    d_normed = d_normed.at[:, :W].add(from_prev).at[:, rows - W :].add(from_next)
    grad_tokens = d_hidden + norm_back(n_one, r_one, d_normed * gain_one)

    vectors = jnp.stack([d_gain_one, d_gain_two, d_router_q, d_router_k, d_router_f])
    for stage in down_a:
        vectors = vectors + flip(vectors, *stage)
    per_device = width // (devices * lax.axis_size("batch"))
    start = (lax.axis_index("batch") * devices + lax.axis_index("seq")) * per_device
    vectors = lax.dynamic_slice_in_dim(vectors, start, per_device, 1).T

    return (
        output,
        grad_tokens,
        d_qkv_light,
        d_outs[:, :IL],
        d_qkv_heavy,
        d_outs[:, IL:],
        d_ff_in,
        d_ff_out,
        d_heavy_ff_in,
        d_heavy_ff_out,
        vectors[:, :2],
        vectors[:, 2:],
    )


def solution(mesh):
    rows = P("batch", "seq", None)
    routes = P("batch", None)
    weight = P(("batch", "seq"), None)
    return jax.shard_map(
        on_device,
        mesh=mesh,
        in_specs=(rows, rows, P("batch"), routes, routes, routes) + (weight,) * 10,
        out_specs=(rows, rows) + (weight,) * 10,
        check_vma=False,
    )
```

```python
import itertools

import jax
import jax.numpy as jnp
from jax import lax
from jax.experimental import pallas as pl
from jax.experimental.pallas import tpu as pltpu
from jax.sharding import PartitionSpec as P

HL = 8
HH = 12
DH = 64
FL = 1024
FH = 4096
W = 128
IL = 512
IH = 768
GROUP = 4

f32 = jnp.float32
bf16 = jnp.bfloat16
fine = lax.Precision.HIGH
eps = 1e-06
GELU_A = 0.7978845608
GELU_B = 0.044715


def bit_stages(axis):
    size, found, step = lax.axis_size(axis), [], 1
    while step < size:
        found.append((axis, step))
        step *= 2
    return found


def own_bit(stage):
    axis, step = stage
    return (lax.axis_index(axis) // step) % 2


def after(values, others):
    values, others = list(values), list(others)
    return list(lax.optimization_barrier(tuple(values) + tuple(others)))[: len(values)]


class Links:
    def __init__(self):
        self.recent = {}

    def queue(self, kind, values):
        recent = self.recent.setdefault(kind, [])
        return after(values, recent[-1]) if recent else values

    def near(self, value):
        groups = [
            list(range(i, i + GROUP)) for i in range(0, lax.axis_size("seq"), GROUP)
        ]
        (value,) = self.queue("near", [value])
        got = lax.all_to_all(value, "seq", 0, 0, axis_index_groups=groups, tiled=True)
        self.recent["near"].append([got])
        return got

    def near_share(self, value):
        return self.near(jnp.broadcast_to(value[None], (GROUP,) + value.shape))

    def far(self, values):
        devices = lax.axis_size("seq")
        sent = self.queue("far", values[1:])
        got = [
            lax.ppermute(v, "seq", [(i, i ^ (GROUP * j)) for i in range(devices)])
            for j, v in enumerate(sent, 1)
        ]
        self.recent["far"].append(got)
        return [values[0]] + got

    def far_share(self, value):
        return self.far([value] * (lax.axis_size("seq") // GROUP))

    def flip(self, values, stage):
        axis, step = stage
        pairs = [(i, i ^ step) for i in range(lax.axis_size(axis))]
        return [lax.ppermute(v, axis, pairs) for v in values]


def far_place():
    return lax.axis_index("seq") // GROUP


def stack_kernel(place, *refs):
    sources, out = refs[:-1], refs[-1]
    for j, source in enumerate(sources):

        @pl.when(pl.program_id(0) == j)
        def _(source=source):
            out[...] = source[...]


def stacked(values, place):
    shape = values[0].shape
    zeros = (0,) * len(shape)
    return pl.pallas_call(
        stack_kernel,
        name="stack",
        grid_spec=pltpu.PrefetchScalarGridSpec(
            num_scalar_prefetch=1,
            grid=(len(values),),
            in_specs=[pl.BlockSpec(shape, lambda j, _: zeros)] * len(values),
            out_specs=pl.BlockSpec((None,) + shape, lambda j, me: (me[0] ^ j,) + zeros),
        ),
        out_shape=jax.ShapeDtypeStruct((len(values),) + shape, values[0].dtype),
        compiler_params=pltpu.CompilerParams(vmem_limit_bytes=40 * 2**20),
        cost_estimate=pl.CostEstimate(
            flops=0, bytes_accessed=4 * values[0].size * len(values), transcendentals=0
        ),
    )(jnp.stack([place]).astype(jnp.int32), *values)


def join_kernel(bit, value, other, out):
    mine = pl.program_id(1) == bit[0]

    @pl.when(mine)
    def _():
        out[...] = value[...]

    @pl.when(jnp.logical_not(mine))
    def _():
        out[...] = other[...]


def joined_halves(value, other, bit, turned):
    steps, inner, rows, width = value.shape
    source = pl.BlockSpec((None, inner, rows, width), lambda i, j, _: (i, 0, 0, 0))
    if turned:
        shape = (2, inner, steps, rows, width)
        target = pl.BlockSpec(
            (None, inner, None, rows, width), lambda i, j, _: (j, 0, i, 0, 0)
        )
    else:
        shape = (2, steps, inner, rows, width)
        target = pl.BlockSpec(
            (None, None, inner, rows, width), lambda i, j, _: (j, i, 0, 0, 0)
        )
    return pl.pallas_call(
        join_kernel,
        name="join",
        grid_spec=pltpu.PrefetchScalarGridSpec(
            num_scalar_prefetch=1,
            grid=(steps, 2),
            in_specs=[source, source],
            out_specs=target,
        ),
        out_shape=jax.ShapeDtypeStruct(shape, value.dtype),
        compiler_params=pltpu.CompilerParams(vmem_limit_bytes=40 * 2**20),
        cost_estimate=pl.CostEstimate(
            flops=0, bytes_accessed=8 * value.size, transcendentals=0
        ),
    )(jnp.stack([bit]).astype(jnp.int32), value, other)


def power_of(block):
    top = jnp.max(jnp.abs(block), axis=-2, keepdims=True)
    return jnp.ceil(jnp.log2(jnp.maximum(top, 1e-30)) + 0.01)


def steps_of(block, power):
    return jnp.floor(block * jnp.exp2(15.0 - power) + 0.5)


def pack_rows(value):
    power = power_of(value)
    extra = jnp.broadcast_to(power, power.shape[:-2] + (8, power.shape[-1]))
    return jnp.concatenate([steps_of(value, power), extra], axis=-2).astype(jnp.int16)


def unpack_rows(packed):
    packed = packed.astype(f32)
    rows = packed.shape[-2] - 8
    return packed[..., :rows, :] * jnp.exp2(packed[..., rows : rows + 1, :] - 15.0)


def power_rows(blocks):
    return -(-blocks // 16) * 16


def packed_blocks(blocks):
    powers = [power_of(block) for block in blocks]
    steps = [steps_of(block, power) for block, power in zip(blocks, powers)]
    powers += [jnp.zeros_like(powers[0])] * (power_rows(len(powers)) - len(powers))
    return jnp.concatenate(steps + powers, axis=0).astype(jnp.int32).astype(jnp.int16)


def block_sum(sources, count, depth):
    totals = [None] * count
    for source in sources:
        steps = source.astype(jnp.int32).astype(f32)
        powers = jnp.exp2(steps[count * depth : count * depth + count] - 15.0)
        for n in range(count):
            block = steps[n * depth : (n + 1) * depth] * powers[n : n + 1]
            totals[n] = block if totals[n] is None else totals[n] + block
    return totals


def give(blocks, layout, place, outs, total):
    if total is None:
        for p, wanted in enumerate(layout):
            outs[0][p] = packed_blocks([blocks[n][low:high] for n, low, high in wanted])
        return
    for p, wanted in enumerate(layout):
        row = 0
        for n, low, high in wanted:
            total[p, row : row + high - low] = blocks[n][low:high]
            row += high - low
    sizes = [high - low for _, low, high in layout[0]]
    for j, out in enumerate(outs):
        rows = total[place ^ j]
        cuts = [sum(sizes[:n]) for n in range(len(sizes) + 1)]
        out[...] = packed_blocks([rows[p:q] for p, q in zip(cuts, cuts[1:])])


def given_form(layout, far, width, tile):
    inner = sum(high - low for _, low, high in layout[0])
    rows = inner + power_rows(len(layout[0]))
    if far:
        return (
            [jax.ShapeDtypeStruct((rows, width), jnp.int16)] * len(layout),
            [pl.BlockSpec((rows, tile), lambda c, _: (0, c))] * len(layout),
            [pltpu.VMEM((len(layout), inner, tile), f32)],
        )
    return (
        [jax.ShapeDtypeStruct((len(layout), rows, width), jnp.int16)],
        [pl.BlockSpec((len(layout), rows, tile), lambda c, _: (0, 0, c))],
        [],
    )


def send_kernel(spans, layout, received, far, place, *refs):
    count = len(spans)
    values, refs = refs[:count], refs[count:]
    others = [None] * count
    if received:
        others, refs = refs[:count], refs[count:]
    outs, total = (refs[:-1], refs[-1]) if far else (refs, None)

    def one(value, other):
        blocks = [value[n] for n in range(value.shape[0])]
        if other is not None:
            got = block_sum([other[...]], len(blocks), blocks[0].shape[0])
            blocks = [p + q for p, q in zip(blocks, got)]
        give(blocks, layout, place[0], outs, total)

    for i, (low, high) in enumerate(spans):
        one_piece = lambda i=i: one(values[i], others[i])
        if count == 1:
            one_piece()
        else:
            pl.when((pl.program_id(0) >= low) & (pl.program_id(0) < high))(one_piece)


def send_form(values, others, layout, far):
    widths = [v.shape[2] for v in values]
    tile = max(t for t in (128, 256, 384, 512) if all(w % t == 0 for w in widths))
    spans, begin = [], 0
    for w in widths:
        spans.append((begin, begin + w // tile))
        begin += w // tile
    received = others[0] is not None

    def spec(shape, span):
        lead = (0,) * (len(shape) - 1)
        return pl.BlockSpec(
            shape[:-1] + (tile,),
            lambda c, _: lead + (jnp.clip(c - span[0], 0, span[1] - span[0] - 1),),
        )

    args = list(values) + (list(others) if received else [])
    shapes, out_specs, scratch = given_form(layout, far, sum(widths), tile)
    got = pl.pallas_call(
        lambda *refs: send_kernel(spans, layout, received, far, *refs),
        name="send",
        grid_spec=pltpu.PrefetchScalarGridSpec(
            num_scalar_prefetch=1,
            grid=(begin,),
            in_specs=[spec(v.shape, s) for v, s in zip(args, spans * 2)],
            out_specs=out_specs,
            scratch_shapes=scratch,
        ),
        out_shape=shapes,
        compiler_params=pltpu.CompilerParams(vmem_limit_bytes=48 * 2**20),
        cost_estimate=pl.CostEstimate(
            flops=20 * sum(v.size for v in values),
            bytes_accessed=8 * sum(v.size for v in values),
            transcendentals=0,
        ),
    )(jnp.stack([far_place()]).astype(jnp.int32), *args)
    return got if far else got[0]


def arrived_kernel(sources, count, depth, layout, far, place, *refs):
    if sources is None:
        packed, refs = [refs[0][n] for n in range(refs[0].shape[0])], refs[1:]
    else:
        packed, refs = [r[...] for r in refs[:sources]], refs[sources:]
    blocks = block_sum(packed, count, depth)
    if layout is None:
        for n, block in enumerate(blocks):
            refs[0][n * depth : (n + 1) * depth] = block
        return
    outs, total = (refs[:-1], refs[-1]) if far else (refs, None)
    give(blocks, layout, place[0], outs, total)


def arrived(packed, count, depth, layout=None, far=False):
    args = list(packed) if isinstance(packed, (list, tuple)) else [packed]
    sources = len(args) if isinstance(packed, (list, tuple)) else None
    width = args[0].shape[-1]
    tile = max(t for t in (128, 256, 384, 512) if width % t == 0)
    if layout is None:
        shapes = [jax.ShapeDtypeStruct((count * depth, width), f32)]
        out_specs, scratch = [pl.BlockSpec((count * depth, tile), lambda c, _: (0, c))], []
    else:
        shapes, out_specs, scratch = given_form(layout, far, width, tile)
    lead = (0,) * (args[0].ndim - 1)
    got = pl.pallas_call(
        lambda *refs: arrived_kernel(sources, count, depth, layout, far, *refs),
        name="arrived",
        grid_spec=pltpu.PrefetchScalarGridSpec(
            num_scalar_prefetch=1,
            grid=(width // tile,),
            in_specs=[
                pl.BlockSpec(a.shape[:-1] + (tile,), lambda c, _: lead + (c,)) for a in args
            ],
            out_specs=out_specs,
            scratch_shapes=scratch,
        ),
        out_shape=shapes,
        compiler_params=pltpu.CompilerParams(vmem_limit_bytes=48 * 2**20),
        cost_estimate=pl.CostEstimate(
            flops=10 * sum(a.size for a in args),
            bytes_accessed=4 * sum(a.size for a in args),
            transcendentals=0,
        ),
    )(jnp.stack([far_place()]).astype(jnp.int32), *args)
    return got if far else got[0]


def grad_kernel(depth, bits, x, y, kept, sent, x_high, x_low):
    @pl.when(pl.program_id(0) == 0)
    def _():
        x_high[...], x_low[...] = split(x[...].T)

    y_high, y_low = split(y[...])
    half = x_high.shape[0] // 2

    def part(which):
        rows = pl.ds(pl.multiple_of(which * half, half), half)
        high = x_high[rows, :]
        return dot_nn(high, y_high) + dot_nn(x_low[rows, :], y_high) + dot_nn(high, y_low)

    kept[...] = part(bits[0])
    other = part(1 - bits[0])
    sent[...] = packed_blocks([other[n : n + depth] for n in range(0, half, depth)])


def grad_split(x, y, bit, depth):
    rows, width = x.shape
    half, columns = width // 2, y.shape[1]
    tile = max(t for t in (128, 256, 512) if columns % t == 0)
    packed = half + power_rows(half // depth)
    return pl.pallas_call(
        lambda *refs: grad_kernel(depth, *refs),
        name="grad",
        grid_spec=pltpu.PrefetchScalarGridSpec(
            num_scalar_prefetch=1,
            grid=(columns // tile,),
            in_specs=[
                pl.BlockSpec((rows, width), lambda c, _: (0, 0)),
                pl.BlockSpec((rows, tile), lambda c, _: (0, c)),
            ],
            out_specs=[
                pl.BlockSpec((half, tile), lambda c, _: (0, c)),
                pl.BlockSpec((packed, tile), lambda c, _: (0, c)),
            ],
            scratch_shapes=[pltpu.VMEM((width, rows), bf16)] * 2,
        ),
        out_shape=[
            jax.ShapeDtypeStruct((half, columns), f32),
            jax.ShapeDtypeStruct((packed, columns), jnp.int16),
        ],
        compiler_params=pltpu.CompilerParams(vmem_limit_bytes=48 * 2**20),
        cost_estimate=pl.CostEstimate(
            flops=6 * rows * width * columns,
            bytes_accessed=4 * (rows * width + rows * columns) + 3 * width * columns,
            transcendentals=0,
        ),
    )(jnp.stack([bit]).astype(jnp.int32), x, y)


def shifted(value, by):
    length = lax.axis_size("seq")
    pairs = [(i, i + by) for i in range(length) if 0 <= i + by < length]
    return unpack_rows(lax.ppermute(pack_rows(value), "seq", pairs))


def product(formula, left_side, right_side):
    return jnp.einsum(
        formula,
        left_side.astype(f32),
        right_side.astype(f32),
        precision=fine,
        preferred_element_type=f32,
    )


def unit_rms(values):
    scale = lax.rsqrt(jnp.mean(values * values, axis=-1, keepdims=True) + eps)
    return values * scale, scale


def norm_back(unit, scale, scaled_grad):
    return scale * (scaled_grad - unit * jnp.mean(scaled_grad * unit, axis=-1, keepdims=True))


def gelu_both(values):
    squared = values * values
    bend = jnp.tanh(GELU_A * (values + GELU_B * squared * values))
    half = 0.5 * (1.0 + bend)
    slope = half + 0.5 * values * (1.0 - bend * bend) * GELU_A * (1.0 + 3.0 * GELU_B * squared)
    return values * half, slope


def local_slots(route_row, row_begin, span_rows, capacity):
    below = jnp.sum((route_row < row_begin).astype(jnp.int32))
    upper = jnp.sum((route_row < row_begin + span_rows).astype(jnp.int32))
    slot = below + jnp.arange(capacity, dtype=jnp.int32)
    index = jnp.arange(route_row.shape[0], dtype=jnp.int32)
    positions = jnp.sum(
        jnp.where(slot[:, None] == index[None, :], route_row[None, :], 0), axis=1
    )
    offsets = positions - row_begin
    matched = (offsets[:, None] == jnp.arange(span_rows, dtype=jnp.int32)[None, :]) & (
        slot < upper
    )[:, None]
    return positions, matched.astype(bf16)


def slot_table(route_row, span_rows, devices, capacity):
    home = route_row // span_rows
    before = jnp.sum((route_row[None, :] < (home * span_rows)[:, None]).astype(jnp.int32), axis=1)
    rank = jnp.arange(route_row.shape[0], dtype=jnp.int32) - before
    place = home * capacity + rank
    return (
        place[:, None] == jnp.arange(devices * capacity, dtype=jnp.int32)[None, :]
    ).astype(bf16)


def split(value):
    high = value.astype(bf16)
    return high, (value - high.astype(f32)).astype(bf16)


def dot_nt(a, b):
    return lax.dot_general(a, b, (((1,), (1,)), ((), ())), preferred_element_type=f32)


def dot_nn(a, b):
    return lax.dot_general(a, b, (((1,), (0,)), ((), ())), preferred_element_type=f32)


def dot_tn(a, b):
    return lax.dot_general(a, b, (((0,), (0,)), ((), ())), preferred_element_type=f32)


def two_heads(value):
    first = lax.broadcasted_iota(jnp.int32, value.shape, 1) < DH
    zero = jnp.zeros_like(value)
    return jnp.concatenate([jnp.where(first, value, zero), jnp.where(first, zero, value)], axis=0)


def one_row_each(value):
    half = value.shape[0] // 2
    first = lax.broadcasted_iota(jnp.int32, (half, value.shape[1]), 1) < DH
    return jnp.where(first, value[:half], value[half:])


def wide_nt(rows_high, rows_low, cols_high, cols_low):
    return dot_nt(
        jnp.concatenate([rows_high, rows_low], axis=1),
        jnp.concatenate([cols_high, cols_high], axis=1),
    ) + dot_nt(rows_high, cols_low)


def wide_nn(a_high, a_low, b_high, b_low):
    columns = b_high.shape[1]
    both = dot_nn(a_high, jnp.concatenate([b_high, b_low], axis=1))
    return both[:, :columns] + both[:, columns:] + dot_nn(a_low, b_high)


def wide_tn(a_high, a_low, b_high, b_low):
    return dot_tn(a_high, b_high) + dot_tn(a_low, b_high) + dot_tn(a_high, b_low)


def pair_probs(query, key_high, key_low, allowed):
    high, low = split(two_heads(query * DH**-0.5))
    scores = wide_nt(key_high, key_low, high, low)
    scores = jnp.where(allowed, scores, -1e30)
    weights = jnp.exp(scores - jnp.max(scores, axis=0, keepdims=True))
    return weights / jnp.sum(weights, axis=0, keepdims=True), high, low


def pair_forward(query, key, value, allowed):
    probs, _, _ = pair_probs(query, *split(key), allowed)
    mixed = wide_tn(*split(value), *split(probs))
    return one_row_each(mixed.T)


def pair_backward(query, key, value, d_out, allowed):
    key_high, key_low = split(key)
    probs, query_high, query_low = pair_probs(query, key_high, key_low, allowed)
    out_high, out_low = split(two_heads(d_out))
    d_value = wide_nn(*split(probs), out_high, out_low)
    d_probs = wide_nt(*split(value), out_high, out_low)
    dots = jnp.sum(probs * d_probs, axis=0, keepdims=True)
    score_high, score_low = split(probs * (d_probs - dots))
    d_key = wide_nn(score_high, score_low, query_high, query_low)
    d_query = wide_tn(key_high, key_low, score_high, score_low)
    return one_row_each(d_query.T) * DH**-0.5, d_key, d_value


def light_allowed(places, seq, block):
    begin, full_len, prefix = places[0], places[1], places[2 + seq]
    shape = (3 * W, 2 * W)
    key_pos = begin + (block - 1) * W + lax.broadcasted_iota(jnp.int32, shape, 0)
    lane = lax.broadcasted_iota(jnp.int32, shape, 1)
    query_pos = begin + block * W + jnp.where(lane < W, lane, lane - W)
    near = jnp.abs(query_pos - key_pos) < W
    inside = (key_pos >= 0) & (key_pos < full_len)
    return near & inside & ((key_pos <= query_pos) | (key_pos < prefix))


def light_forward_kernel(places, q, kv, out):
    seq, block = pl.program_id(0), pl.program_id(1)
    allowed = light_allowed(places, seq, block)
    span = pl.ds(pl.multiple_of(block * W, W), 3 * W)
    for pair in range(HL // 2):
        lanes = slice(2 * DH * pair, 2 * DH * (pair + 1))
        values = slice(IL + 2 * DH * pair, IL + 2 * DH * (pair + 1))
        out[0, :, lanes] = pair_forward(
            q[0, :, lanes], kv[0, span, lanes], kv[0, span, values], allowed
        )


def light_backward_kernel(places, q, kv, d_out, d_q, d_kv):
    seq, block = pl.program_id(0), pl.program_id(1)
    allowed = light_allowed(places, seq, block)
    span = pl.ds(pl.multiple_of(block * W, W), 3 * W)

    @pl.when(block == 0)
    def _():
        d_kv[...] = jnp.zeros_like(d_kv)

    for pair in range(HL // 2):
        lanes = slice(2 * DH * pair, 2 * DH * (pair + 1))
        values = slice(IL + 2 * DH * pair, IL + 2 * DH * (pair + 1))
        d_query, d_key, d_value = pair_backward(
            q[0, :, lanes], kv[0, span, lanes], kv[0, span, values], d_out[0, :, lanes], allowed
        )
        d_q[0, :, lanes] = d_query
        d_kv[0, span, lanes] += d_key
        d_kv[0, span, values] += d_value


def light_call(kernel, places, args, out_shapes, flops):
    seqs, rows, _ = args[0].shape

    def spec(shape):
        if shape[1] == rows:
            return pl.BlockSpec((1, W, shape[2]), lambda s, b, _: (s, b, 0))
        return pl.BlockSpec((1,) + shape[1:], lambda s, b, _: (s, 0, 0))

    return pl.pallas_call(
        kernel,
        name=kernel.__name__,
        grid_spec=pltpu.PrefetchScalarGridSpec(
            num_scalar_prefetch=1,
            grid=(seqs, rows // W),
            in_specs=[spec(a.shape) for a in args],
            out_specs=[spec(o) for o in out_shapes],
        ),
        out_shape=[jax.ShapeDtypeStruct(o, f32) for o in out_shapes],
        compiler_params=pltpu.CompilerParams(vmem_limit_bytes=48 * 2**20),
        cost_estimate=pl.CostEstimate(flops=flops, bytes_accessed=2**23, transcendentals=2**21),
    )(places, *args)


def heavy_allowed(prefix, key_pos, query_pos):
    return (key_pos <= query_pos) | (key_pos < prefix)


def heavy_forward_kernel(places, key_pos, query_pos, q, kv, out):
    allowed = heavy_allowed(places[2 + pl.program_id(0)], key_pos[0], query_pos[0])
    for pair in range(HH // 2):
        lanes = slice(2 * DH * pair, 2 * DH * (pair + 1))
        values = slice(IH + 2 * DH * pair, IH + 2 * DH * (pair + 1))
        out[0, :, lanes] = pair_forward(
            q[0, :, lanes], kv[0, :, lanes], kv[0, :, values], allowed
        )


def heavy_backward_kernel(places, key_pos, query_pos, q, kv, d_out, d_q, d_kv):
    allowed = heavy_allowed(places[2 + pl.program_id(0)], key_pos[0], query_pos[0])
    for pair in range(HH // 2):
        lanes = slice(2 * DH * pair, 2 * DH * (pair + 1))
        values = slice(IH + 2 * DH * pair, IH + 2 * DH * (pair + 1))
        d_query, d_key, d_value = pair_backward(
            q[0, :, lanes], kv[0, :, lanes], kv[0, :, values], d_out[0, :, lanes], allowed
        )
        d_q[0, :, lanes] = d_query
        d_kv[0, :, lanes] = d_key
        d_kv[0, :, values] = d_value


def heavy_call(kernel, places, args, out_shapes, flops):
    def spec(shape):
        return pl.BlockSpec((1,) + shape[1:], lambda s, _: (s, 0, 0))

    return pl.pallas_call(
        kernel,
        name=kernel.__name__,
        grid_spec=pltpu.PrefetchScalarGridSpec(
            num_scalar_prefetch=1,
            grid=(args[0].shape[0],),
            in_specs=[spec(a.shape) for a in args],
            out_specs=[spec(o) for o in out_shapes],
        ),
        out_shape=[jax.ShapeDtypeStruct(o, f32) for o in out_shapes],
        compiler_params=pltpu.CompilerParams(vmem_limit_bytes=48 * 2**20),
        cost_estimate=pl.CostEstimate(flops=flops, bytes_accessed=2**23, transcendentals=2**20),
    )(places, *args)


def on_device(
    tokens,
    cotangent,
    prefix_len,
    query_routes,
    key_routes,
    ffn_routes,
    light_qkv,
    light_out,
    heavy_qkv,
    heavy_out,
    light_ff_in,
    light_ff_out,
    heavy_ff_in,
    heavy_ff_out,
    gains,
    routers,
):
    seqs, rows, width = tokens.shape
    devices = lax.axis_size("seq")
    row_begin = lax.axis_index("seq") * rows
    full_len = rows * devices
    capacity = rows // 4
    units = FH // GROUP

    batch_bits = bit_stages("batch")
    far = devices // GROUP
    device_rows = width // (devices * lax.axis_size("batch"))
    core = lax.axis_index("batch") % 2
    tiled = len(batch_bits) == 1 and device_rows % 8 == 0
    links = Links()

    def joined(*pieces):
        return jnp.concatenate(pieces, axis=1)

    def flat(value):
        return value.reshape(-1, value.shape[-1])

    def chip_gather(value, turned):
        for stage in batch_bits:
            (other,) = links.flip([value], stage)
            value = joined_halves(value, other, own_bit(stage), turned)
            value = value.reshape((value.shape[0] * value.shape[1],) + value.shape[2:])
            turned = False
        return flat(value)

    class Sum:
        def __init__(self, pieces, depth, first):
            self.depth, self.first, self.value = depth, first, None
            if not tiled:
                value = joined(
                    *[p if not isinstance(p, tuple) else product("rd,re->de", *p) for p in pieces]
                )
                value = value.reshape((2,) * len(batch_bits) + (-1, value.shape[1]))
                for stage in batch_bits[::-1]:
                    mine = own_bit(stage)
                    sent = lax.dynamic_index_in_dim(value, 1 - mine, 0, keepdims=False)
                    kept = lax.dynamic_index_in_dim(value, mine, 0, keepdims=False)
                    value = kept + links.flip([sent], stage)[0]
                self.value = value.reshape(far, GROUP, device_rows, -1)
                return
            kept, sent = [], []
            for p in pieces:
                if isinstance(p, tuple):
                    mine, other = grad_split(*p, core, depth)
                else:
                    p = p.reshape(2, -1, depth, p.shape[1])
                    mine = lax.dynamic_index_in_dim(p, core, 0, keepdims=False)
                    other = lax.dynamic_index_in_dim(p, 1 - core, 0, keepdims=False)
                    power = power_of(other)
                    spare = jnp.zeros((power_rows(len(other)) - len(other), p.shape[3]), f32)
                    other = jnp.concatenate(
                        [flat(steps_of(other, power)), flat(power), spare], axis=0
                    ).astype(jnp.int16)
                kept.append(mine.reshape(-1, depth, mine.shape[-1]))
                sent.append(other)
            got = links.flip(sent, batch_bits[0])
            if first == "near":
                layout = [[(f * GROUP + p, 0, depth) for f in range(far)] for p in range(GROUP)]
            else:
                layout = [[(f, 0, depth)] for f in range(far)]
            self.sent = send_form(kept, got, layout, first == "far")

        def near(self):
            if not tiled:
                if self.first == "near":
                    self.value = jnp.sum(links.near(jnp.swapaxes(self.value, 0, 1)), axis=0)
                else:
                    self.value = links.near(self.value)
                return
            self.value = links.near(self.sent)
            if self.first == "near":
                layout = [[(f, 0, self.depth)] for f in range(far)]
                self.sent = arrived(self.value, far, self.depth, layout, True)

        def far(self):
            if not tiled:
                parts = [
                    lax.dynamic_index_in_dim(self.value, far_place() ^ j, 0, keepdims=False)
                    for j in range(far)
                ]
                self.value = sum(links.far(parts))
                return
            self.value = links.far(self.sent)
            if self.first == "far":
                layout = [
                    [(0, p * device_rows, (p + 1) * device_rows)] for p in range(GROUP)
                ]
                self.sent = arrived(self.value, 1, self.depth, layout)

        def result(self):
            if not tiled:
                return self.value
            if self.first == "near":
                return arrived(self.value, 1, self.depth)
            value = self.value.astype(f32)
            power = value[:, device_rows : device_rows + 1]
            return value[:, :device_rows] * jnp.exp2(power - 15.0)

    n_one, r_one = unit_rms(tokens)
    def picker(route_row):
        return local_slots(route_row, row_begin, rows, capacity)

    query_at, query_pick = jax.vmap(picker)(query_routes)
    _, key_pick = jax.vmap(picker)(key_routes)
    _, ffn_pick = jax.vmap(picker)(ffn_routes)
    table = jax.vmap(lambda r: slot_table(r, rows, devices, capacity))(key_routes)

    picked = product("sct,std->scd", jnp.concatenate([query_pick, key_pick], axis=1), n_one)
    query_unit, key_unit_own = picked[:, :capacity], picked[:, capacity:]

    spare = jnp.zeros((gains.shape[0], 128 - 5), bf16)
    before = shifted(tokens[:, rows - W :], 1)
    after_rows = shifted(tokens[:, :W], -1)
    first = links.far_share(joined(light_qkv, heavy_qkv, gains, routers, spare))
    key_far = links.far_share(pack_rows(key_unit_own))
    first = links.near_share(stacked(first, far_place()))
    key_far = stacked(key_far, far_place())
    first, key_far = after([first, key_far], [])

    def unit_parts(value):
        return jnp.swapaxes(value.reshape(value.shape[0], -1, units), 0, 1)

    big = jnp.concatenate(
        [
            unit_parts(heavy_ff_in).reshape(2, GROUP, device_rows, units),
            unit_parts(heavy_ff_out).reshape(1, GROUP, device_rows, units),
        ]
    )
    big = jnp.swapaxes(big, 0, 1).transpose(0, 2, 1, 3).reshape(GROUP, device_rows, 3 * units)
    big = links.near(big)
    first = chip_gather(first, True)
    (first,) = after([first], [big])
    keys = links.near_share(key_far)
    later_far = links.far_share(joined(light_out, heavy_out, light_ff_out, light_ff_in))
    big = links.far_share(big)
    qkv_light, qkv_heavy = first[:, : 3 * IL], first[:, 3 * IL : 3 * IL + 3 * IH]
    small = first[:, 3 * (IL + IH) :].astype(f32)
    gain_one, gain_two = small[:, 0], small[:, 1]
    router_q, router_k, router_f = small[:, 2], small[:, 3], small[:, 4]

    key_slots = unpack_rows(keys.transpose(2, 1, 0, 3, 4)).reshape(seqs, -1, width)
    cot_own = product("sct,std->scd", ffn_pick, cotangent)

    n_ext = unit_rms(jnp.concatenate([before, tokens, after_rows], axis=1))[0]
    normed_ext = n_ext * gain_one
    normed = n_one * gain_one
    light_q = product("std,de->ste", normed, qkv_light[:, :IL])
    light_kv = product("std,de->ste", normed_ext, qkv_light[:, IL:])
    places = jnp.concatenate(
        [jnp.stack([row_begin, jnp.int32(full_len)]), prefix_len]
    ).astype(jnp.int32)
    later = links.near_share(stacked(after(later_far, [light_kv]), far_place()))
    (attended,) = light_call(
        light_forward_kernel, places, (light_q, light_kv), (light_q.shape,), 2**33
    )
    query_rows = query_unit * gain_one
    key_unit = product("skp,spd->skd", table, key_slots)
    key_rows = key_unit * gain_one
    query_score = jax.nn.sigmoid(jnp.sum(query_rows * router_q, axis=-1))
    key_score = jax.nn.sigmoid(jnp.sum(key_rows * router_k, axis=-1))
    heavy_q = product("scd,di->sci", query_rows, qkv_heavy[:, :IH])
    heavy_kv = product("skd,de->ske", key_rows, qkv_heavy[:, IH:])
    heavy_v_raw = heavy_kv[..., IH:]
    heavy_kv = jnp.concatenate(
        [heavy_kv[..., :IH], heavy_v_raw * key_score[..., None]], axis=-1
    )
    key_column = key_routes[:, :, None]
    query_row = jnp.concatenate([query_at, query_at], axis=1)[:, None, :]
    (heavy_mixed,) = heavy_call(
        heavy_forward_kernel,
        places,
        (key_column, query_row, heavy_q, heavy_kv),
        (heavy_q.shape,),
        2**33,
    )
    big = stacked(after(big, [attended]), far_place())
    later = chip_gather(later, True)
    out_light, out_heavy = later[:, :IL], later[:, IL : IL + IH]
    ff_out, ff_in = later[:, IL + IH : IL + IH + FL], later[:, IL + IH + FL :]
    light_branch = product("sti,di->std", attended, out_light)
    big = chip_gather(big, False)
    big_in, big_out = big[:, : 2 * units], big[:, 2 * units :]

    heavy_plain = product("sci,di->scd", heavy_mixed, out_heavy)
    heavy_rows = heavy_plain * query_score[..., None]
    hidden = tokens + light_branch + product("sct,scd->std", query_pick, heavy_rows)

    n_two, r_two = unit_rms(hidden)
    second = n_two * gain_two
    ffn_own = product("sct,std->scd", ffn_pick, second)
    routed = unpack_rows(links.near_share(pack_rows(jnp.stack([ffn_own, cot_own]))))
    ffn_rows, cot_rows = (flat(routed[:, i]) for i in range(2))
    gate_up = product("std,de->ste", second, ff_in)
    gate, up = gate_up[..., :FL], gate_up[..., FL:]
    gate_act, gate_slope = gelu_both(gate)
    light_act = gate_act * up
    light_ff = product("stf,df->std", light_act, ff_out)
    d_act = product("std,df->stf", cotangent, ff_out)
    d_gate_up = jnp.concatenate([d_act * up * gate_slope, d_act * gate_act], axis=-1)
    d_second = product("ste,de->std", d_gate_up, ff_in)
    d_ff = Sum(
        [(flat(cotangent), flat(light_act)), (flat(second), flat(d_gate_up))], device_rows, "near"
    )

    ffn_score = jax.nn.sigmoid(jnp.sum(ffn_rows * router_f, axis=-1, keepdims=True))
    big_gate_up = product("rd,de->re", ffn_rows, big_in)
    big_gate, big_up = big_gate_up[:, :units], big_gate_up[:, units:]
    big_act, big_slope = gelu_both(big_gate)
    big_mix = big_act * big_up
    cot_mix = product("rd,df->rf", cot_rows, big_out)
    d_score = jnp.sum(cot_mix * big_mix, axis=-1, keepdims=True)
    d_score_in = d_score * ffn_score * (1.0 - ffn_score)
    d_mix = cot_mix * ffn_score
    d_big = jnp.concatenate([d_mix * big_up * big_slope, d_mix * big_act], axis=-1)
    d_ffn_rows = product("re,de->rd", d_big, big_in) + d_score_in * router_f
    d_router_f = jnp.sum(d_score_in * ffn_rows, axis=0)

    big_rows = product("rf,df->rd", big_mix, big_out) * ffn_score
    both = jnp.stack([d_ffn_rows, big_rows]).reshape(-1, capacity, width)
    layout = [
        [((m * GROUP + p) * seqs + i, 0, capacity) for m in range(2) for i in range(seqs)]
        for p in range(GROUP)
    ]
    back = arrived(
        links.near(send_form([both], [None], layout, False)), 2 * seqs, capacity
    ).reshape(2, seqs, capacity, width)
    ffn_own, out_own = back[0], back[1]
    d_big_all = Sum(
        [(ffn_rows, d_big), (cot_rows, big_mix * ffn_score)], GROUP * device_rows, "far"
    )
    d_big_all.far()
    d_ff.near()

    output = hidden + light_ff + product("sct,scd->std", ffn_pick, out_own)
    d_second = d_second + product("sct,scd->std", ffn_pick, ffn_own)
    d_gain_two = jnp.sum(d_second * n_two, axis=(0, 1))
    d_hidden = cotangent + norm_back(n_two, r_two, d_second * gain_two)

    d_heavy_rows = product("sct,std->scd", query_pick, d_hidden)
    d_query_score = jnp.sum(d_heavy_rows * heavy_plain, axis=-1)
    d_plain = d_heavy_rows * query_score[..., None]
    d_mixed = product("scd,di->sci", d_plain, out_heavy)
    d_attended = product("std,di->sti", d_hidden, out_light)
    (d_mixed,) = after([d_mixed], list(d_big_all.sent) if tiled else [d_big_all.value])
    d_hq, d_hkv = heavy_call(
        heavy_backward_kernel,
        places,
        (key_column, query_row, heavy_q, heavy_kv, d_mixed),
        (heavy_q.shape, heavy_kv.shape),
        2**34,
    )
    d_hq, d_hkv = after([d_hq, d_hkv], [d_ff.value])
    d_hv = d_hkv[..., IH:]
    d_key_score = jnp.sum(d_hv * heavy_v_raw, axis=-1)
    d_key_in = d_key_score * key_score * (1.0 - key_score)
    d_query_in = d_query_score * query_score * (1.0 - query_score)
    d_kv = jnp.concatenate([d_hkv[..., :IH], d_hv * key_score[..., None]], axis=-1)
    d_key_rows = product("ske,de->skd", d_kv, qkv_heavy[:, IH:]) + d_key_in[..., None] * router_k
    d_query_rows = (
        product("sci,di->scd", d_hq, qkv_heavy[:, :IH]) + d_query_in[..., None] * router_q
    )
    d_router_k = jnp.sum(d_key_in[..., None] * key_rows, axis=(0, 1))
    d_router_q = jnp.sum(d_query_in[..., None] * query_rows, axis=(0, 1))
    d_key_slots = product("skp,skd->spd", table, d_key_rows)
    layout = [
        [((i * far + f) * GROUP + p, 0, capacity) for f in range(far) for i in range(seqs)]
        for p in range(GROUP)
    ]
    key_sent = send_form([d_key_slots.reshape(-1, capacity, width)], [None], layout, False)
    key_near = links.near(key_sent)
    d_ff.far()
    layout = [[(f * seqs + i, 0, capacity) for i in range(seqs)] for f in range(far)]
    d_key_own = links.far(arrived(key_near, far * seqs, capacity, layout, True))
    d_key_own = arrived(d_key_own, seqs, capacity).reshape(seqs, capacity, width)
    d_mid = Sum(
        [
            (flat(d_hidden), flat(attended)),
            (flat(d_plain), flat(heavy_mixed)),
            (flat(query_rows), flat(d_hq)),
            (flat(key_rows), flat(d_kv)),
        ],
        device_rows,
        "near",
    )
    (d_attended,) = after([d_attended], [d_mid.sent if tiled else d_mid.value])

    d_lq, d_lkv = light_call(
        light_backward_kernel,
        places,
        (light_q, light_kv, d_attended),
        (light_q.shape, light_kv.shape),
        2**34,
    )
    d_lq, d_lkv = after([d_lq, d_lkv], [key_near])
    d_ext = product("ste,de->std", d_lkv, qkv_light[:, IL:])
    from_next = shifted(d_ext[:, :W], -1)
    from_prev = shifted(d_ext[:, W + rows :], 1)
    d_own = product("ste,de->std", d_lq, qkv_light[:, :IL]) + product(
        "sct,scd->std", query_pick, d_query_rows
    )
    d_gain_one = (
        jnp.sum(d_ext * n_ext, axis=(0, 1))
        + jnp.sum(d_own * n_one, axis=(0, 1))
        + jnp.sum(d_key_rows * key_unit, axis=(0, 1))
    )
    edges = jnp.pad(from_prev, ((0, 0), (0, rows - W), (0, 0))) + jnp.pad(
        from_next, ((0, 0), (rows - W, 0), (0, 0))
    )
    vectors = jnp.stack([d_gain_one, d_gain_two, d_router_q, d_router_k, d_router_f])
    vectors = jnp.pad(vectors, ((0, 128 - 5), (0, 0))).T
    last = Sum(
        [(flat(normed), flat(d_lq)), (flat(normed_ext), flat(d_lkv)), vectors],
        device_rows,
        "near",
    )
    d_mid.near()
    last.near()
    d_mid.far()
    last.far()
    d_big_all.near()
    d_ff, d_mid, last = d_ff.result(), d_mid.result(), last.result()
    d_big_all = d_big_all.result()
    vectors = last[:, 3 * IL :]

    def spread(value):
        return jnp.swapaxes(value, 0, 1).reshape(value.shape[1], -1)

    d_heavy_ff_in = joined(
        spread(d_big_all[..., :units]), spread(d_big_all[..., units : 2 * units])
    )
    d_heavy_ff_out = spread(d_big_all[..., 2 * units :])

    d_normed = (
        d_own
        + d_ext[:, W : W + rows]
        + edges
        + product("sct,scd->std", key_pick, d_key_own)
    )
    grad_tokens = d_hidden + norm_back(n_one, r_one, d_normed * gain_one)

    return (
        output,
        grad_tokens,
        last[:, : 3 * IL],
        d_mid[:, :IL],
        d_mid[:, IL + IH :],
        d_mid[:, IL : IL + IH],
        d_ff[:, FL:],
        d_ff[:, :FL],
        d_heavy_ff_in,
        d_heavy_ff_out,
        vectors[:, :2],
        vectors[:, 2:5],
    )


def solution(mesh):
    rows = P("batch", "seq", None)
    routes = P("batch", None)
    weight = P(("batch", "seq"), None)
    return jax.shard_map(
        on_device,
        mesh=mesh,
        in_specs=(rows, rows, P("batch"), routes, routes, routes) + (weight,) * 10,
        out_specs=(rows, rows) + (weight,) * 10,
        check_vma=False,
    )
```

```python
import itertools

import jax
import jax.numpy as jnp
from jax import lax
from jax.experimental import pallas as pl
from jax.experimental.pallas import tpu as pltpu
from jax.sharding import PartitionSpec as P

HL = 8
HH = 12
DH = 64
FL = 1024
FH = 4096
W = 128
IL = 512
IH = 768
GROUP = 4

f32 = jnp.float32
bf16 = jnp.bfloat16
fine = lax.Precision.HIGH
eps = 1e-06
GELU_A = 0.7978845608
GELU_B = 0.044715


def bit_stages(axis):
    size, found, step = lax.axis_size(axis), [], 1
    while step < size:
        found.append((axis, step))
        step *= 2
    return found


def own_bit(stage):
    axis, step = stage
    return (lax.axis_index(axis) // step) % 2


def after(values, others):
    values, others = list(values), list(others)
    return list(lax.optimization_barrier(tuple(values) + tuple(others)))[: len(values)]


class Links:
    def __init__(self):
        self.recent = {}

    def queue(self, kind, values):
        recent = self.recent.setdefault(kind, [])
        return after(values, recent[-1]) if recent else values

    def near(self, value):
        groups = [
            list(range(i, i + GROUP)) for i in range(0, lax.axis_size("seq"), GROUP)
        ]
        (value,) = self.queue("near", [value])
        got = lax.all_to_all(value, "seq", 0, 0, axis_index_groups=groups, tiled=True)
        self.recent["near"].append([got])
        return got

    def near_share(self, value):
        return self.near(jnp.broadcast_to(value[None], (GROUP,) + value.shape))

    def far(self, values):
        devices = lax.axis_size("seq")
        sent = self.queue("far", values[1:])
        got = [
            lax.ppermute(v, "seq", [(i, i ^ (GROUP * j)) for i in range(devices)])
            for j, v in enumerate(sent, 1)
        ]
        self.recent["far"].append(got)
        return [values[0]] + got

    def far_share(self, value):
        return self.far([value] * (lax.axis_size("seq") // GROUP))

    def flip(self, values, stage):
        axis, step = stage
        pairs = [(i, i ^ step) for i in range(lax.axis_size(axis))]
        return [lax.ppermute(v, axis, pairs) for v in values]


def far_place():
    return lax.axis_index("seq") // GROUP


def stack_kernel(place, *refs):
    sources, out = refs[:-1], refs[-1]
    for j, source in enumerate(sources):

        @pl.when(pl.program_id(0) == j)
        def _(source=source):
            out[...] = source[...]


def stacked(values, place):
    shape = values[0].shape
    zeros = (0,) * len(shape)
    return pl.pallas_call(
        stack_kernel,
        name="stack",
        grid_spec=pltpu.PrefetchScalarGridSpec(
            num_scalar_prefetch=1,
            grid=(len(values),),
            in_specs=[pl.BlockSpec(shape, lambda j, _: zeros)] * len(values),
            out_specs=pl.BlockSpec((None,) + shape, lambda j, me: (me[0] ^ j,) + zeros),
        ),
        out_shape=jax.ShapeDtypeStruct((len(values),) + shape, values[0].dtype),
        compiler_params=pltpu.CompilerParams(vmem_limit_bytes=40 * 2**20),
        cost_estimate=pl.CostEstimate(
            flops=0, bytes_accessed=4 * values[0].size * len(values), transcendentals=0
        ),
    )(jnp.stack([place]).astype(jnp.int32), *values)


def join_kernel(bit, value, other, out):
    mine = pl.program_id(1) == bit[0]

    @pl.when(mine)
    def _():
        out[...] = value[...]

    @pl.when(jnp.logical_not(mine))
    def _():
        out[...] = other[...]


def joined_halves(value, other, bit, turned):
    steps, inner, rows, width = value.shape
    source = pl.BlockSpec((None, inner, rows, width), lambda i, j, _: (i, 0, 0, 0))
    if turned:
        shape = (2, inner, steps, rows, width)
        target = pl.BlockSpec(
            (None, inner, None, rows, width), lambda i, j, _: (j, 0, i, 0, 0)
        )
    else:
        shape = (2, steps, inner, rows, width)
        target = pl.BlockSpec(
            (None, None, inner, rows, width), lambda i, j, _: (j, i, 0, 0, 0)
        )
    return pl.pallas_call(
        join_kernel,
        name="join",
        grid_spec=pltpu.PrefetchScalarGridSpec(
            num_scalar_prefetch=1,
            grid=(steps, 2),
            in_specs=[source, source],
            out_specs=target,
        ),
        out_shape=jax.ShapeDtypeStruct(shape, value.dtype),
        compiler_params=pltpu.CompilerParams(vmem_limit_bytes=40 * 2**20),
        cost_estimate=pl.CostEstimate(
            flops=0, bytes_accessed=8 * value.size, transcendentals=0
        ),
    )(jnp.stack([bit]).astype(jnp.int32), value, other)


def power_of(block):
    top = jnp.max(jnp.abs(block), axis=-2, keepdims=True)
    return jnp.ceil(jnp.log2(jnp.maximum(top, 1e-30)) + 0.01)


def steps_of(block, power):
    return jnp.floor(block * jnp.exp2(15.0 - power) + 0.5)


def pack_rows(value):
    power = power_of(value)
    extra = jnp.broadcast_to(power, power.shape[:-2] + (8, power.shape[-1]))
    return jnp.concatenate([steps_of(value, power), extra], axis=-2).astype(jnp.int16)


def unpack_rows(packed):
    packed = packed.astype(f32)
    rows = packed.shape[-2] - 8
    return packed[..., :rows, :] * jnp.exp2(packed[..., rows : rows + 1, :] - 15.0)


def power_rows(blocks):
    return -(-blocks // 16) * 16


def packed_blocks(blocks):
    powers = [power_of(block) for block in blocks]
    steps = [steps_of(block, power) for block, power in zip(blocks, powers)]
    powers += [jnp.zeros_like(powers[0])] * (power_rows(len(powers)) - len(powers))
    return jnp.concatenate(steps + powers, axis=0).astype(jnp.int32).astype(jnp.int16)


def block_sum(sources, count, depth):
    totals = [None] * count
    for source in sources:
        steps = source.astype(jnp.int32).astype(f32)
        powers = jnp.exp2(steps[count * depth : count * depth + count] - 15.0)
        for n in range(count):
            block = steps[n * depth : (n + 1) * depth] * powers[n : n + 1]
            totals[n] = block if totals[n] is None else totals[n] + block
    return totals


def give(blocks, layout, place, outs, total):
    if total is None:
        for p, wanted in enumerate(layout):
            outs[0][p] = packed_blocks([blocks[n][low:high] for n, low, high in wanted])
        return
    for p, wanted in enumerate(layout):
        row = 0
        for n, low, high in wanted:
            total[p, row : row + high - low] = blocks[n][low:high]
            row += high - low
    sizes = [high - low for _, low, high in layout[0]]
    for j, out in enumerate(outs):
        rows = total[place ^ j]
        cuts = [sum(sizes[:n]) for n in range(len(sizes) + 1)]
        out[...] = packed_blocks([rows[p:q] for p, q in zip(cuts, cuts[1:])])


def given_form(layout, far, width, tile):
    inner = sum(high - low for _, low, high in layout[0])
    rows = inner + power_rows(len(layout[0]))
    if far:
        return (
            [jax.ShapeDtypeStruct((rows, width), jnp.int16)] * len(layout),
            [pl.BlockSpec((rows, tile), lambda c, _: (0, c))] * len(layout),
            [pltpu.VMEM((len(layout), inner, tile), f32)],
        )
    return (
        [jax.ShapeDtypeStruct((len(layout), rows, width), jnp.int16)],
        [pl.BlockSpec((len(layout), rows, tile), lambda c, _: (0, 0, c))],
        [],
    )


def send_kernel(spans, layout, received, far, place, *refs):
    count = len(spans)
    values, refs = refs[:count], refs[count:]
    others = [None] * count
    if received:
        others, refs = refs[:count], refs[count:]
    outs, total = (refs[:-1], refs[-1]) if far else (refs, None)

    def one(value, other):
        blocks = [value[n] for n in range(value.shape[0])]
        if other is not None:
            parts = [other[...]] if len(other.shape) == 2 else [other[g] for g in range(other.shape[0])]
            each = len(blocks) // len(parts)
            got = [q for part in parts for q in block_sum([part], each, blocks[0].shape[0])]
            blocks = [p + q for p, q in zip(blocks, got)]
        give(blocks, layout, place[0], outs, total)

    for i, (low, high) in enumerate(spans):
        one_piece = lambda i=i: one(values[i], others[i])
        if count == 1:
            one_piece()
        else:
            pl.when((pl.program_id(0) >= low) & (pl.program_id(0) < high))(one_piece)


def send_form(values, others, layout, far):
    widths = [v.shape[2] for v in values]
    tile = max(t for t in (128, 256, 384, 512) if all(w % t == 0 for w in widths))
    spans, begin = [], 0
    for w in widths:
        spans.append((begin, begin + w // tile))
        begin += w // tile
    received = others[0] is not None

    def spec(shape, span):
        lead = (0,) * (len(shape) - 1)
        return pl.BlockSpec(
            shape[:-1] + (tile,),
            lambda c, _: lead + (jnp.clip(c - span[0], 0, span[1] - span[0] - 1),),
        )

    args = list(values) + (list(others) if received else [])
    shapes, out_specs, scratch = given_form(layout, far, sum(widths), tile)
    got = pl.pallas_call(
        lambda *refs: send_kernel(spans, layout, received, far, *refs),
        name="send",
        grid_spec=pltpu.PrefetchScalarGridSpec(
            num_scalar_prefetch=1,
            grid=(begin,),
            in_specs=[spec(v.shape, s) for v, s in zip(args, spans * 2)],
            out_specs=out_specs,
            scratch_shapes=scratch,
        ),
        out_shape=shapes,
        compiler_params=pltpu.CompilerParams(vmem_limit_bytes=48 * 2**20),
        cost_estimate=pl.CostEstimate(
            flops=20 * sum(v.size for v in values),
            bytes_accessed=8 * sum(v.size for v in values),
            transcendentals=0,
        ),
    )(jnp.stack([far_place()]).astype(jnp.int32), *args)
    return got if far else got[0]


def arrived_kernel(sources, count, depth, layout, far, place, *refs):
    if sources is None:
        packed, refs = [refs[0][n] for n in range(refs[0].shape[0])], refs[1:]
    else:
        packed, refs = [r[...] for r in refs[:sources]], refs[sources:]
    blocks = block_sum(packed, count, depth)
    if layout is None:
        for n, block in enumerate(blocks):
            refs[0][n * depth : (n + 1) * depth] = block
        return
    outs, total = (refs[:-1], refs[-1]) if far else (refs, None)
    give(blocks, layout, place[0], outs, total)


def arrived(packed, count, depth, layout=None, far=False):
    args = list(packed) if isinstance(packed, (list, tuple)) else [packed]
    sources = len(args) if isinstance(packed, (list, tuple)) else None
    width = args[0].shape[-1]
    tile = max(t for t in (128, 256, 384, 512) if width % t == 0)
    if layout is None:
        shapes = [jax.ShapeDtypeStruct((count * depth, width), f32)]
        out_specs, scratch = [pl.BlockSpec((count * depth, tile), lambda c, _: (0, c))], []
    else:
        shapes, out_specs, scratch = given_form(layout, far, width, tile)
    lead = (0,) * (args[0].ndim - 1)
    got = pl.pallas_call(
        lambda *refs: arrived_kernel(sources, count, depth, layout, far, *refs),
        name="arrived",
        grid_spec=pltpu.PrefetchScalarGridSpec(
            num_scalar_prefetch=1,
            grid=(width // tile,),
            in_specs=[
                pl.BlockSpec(a.shape[:-1] + (tile,), lambda c, _: lead + (c,)) for a in args
            ],
            out_specs=out_specs,
            scratch_shapes=scratch,
        ),
        out_shape=shapes,
        compiler_params=pltpu.CompilerParams(vmem_limit_bytes=48 * 2**20),
        cost_estimate=pl.CostEstimate(
            flops=10 * sum(a.size for a in args),
            bytes_accessed=4 * sum(a.size for a in args),
            transcendentals=0,
        ),
    )(jnp.stack([far_place()]).astype(jnp.int32), *args)
    return got if far else got[0]


def grad_kernel(depth, bits, x, y, kept, sent, x_high, x_low):
    @pl.when(pl.program_id(0) == 0)
    def _():
        x_high[...], x_low[...] = split(x[...].T)

    y_high, y_low = split(y[...])
    half = x_high.shape[0] // 2

    def part(which):
        rows = pl.ds(pl.multiple_of(which * half, half), half)
        high = x_high[rows, :]
        return dot_nn(high, y_high) + dot_nn(x_low[rows, :], y_high) + dot_nn(high, y_low)

    kept[...] = part(bits[0])
    other = part(1 - bits[0])
    sent[...] = packed_blocks([other[n : n + depth] for n in range(0, half, depth)])


def grad_split(x, y, bit, depth):
    rows, width = x.shape
    half, columns = width // 2, y.shape[1]
    tile = max(t for t in (128, 256, 512) if columns % t == 0)
    packed = half + power_rows(half // depth)
    return pl.pallas_call(
        lambda *refs: grad_kernel(depth, *refs),
        name="grad",
        grid_spec=pltpu.PrefetchScalarGridSpec(
            num_scalar_prefetch=1,
            grid=(columns // tile,),
            in_specs=[
                pl.BlockSpec((rows, width), lambda c, _: (0, 0)),
                pl.BlockSpec((rows, tile), lambda c, _: (0, c)),
            ],
            out_specs=[
                pl.BlockSpec((half, tile), lambda c, _: (0, c)),
                pl.BlockSpec((packed, tile), lambda c, _: (0, c)),
            ],
            scratch_shapes=[pltpu.VMEM((width, rows), bf16)] * 2,
        ),
        out_shape=[
            jax.ShapeDtypeStruct((half, columns), f32),
            jax.ShapeDtypeStruct((packed, columns), jnp.int16),
        ],
        compiler_params=pltpu.CompilerParams(vmem_limit_bytes=48 * 2**20),
        cost_estimate=pl.CostEstimate(
            flops=6 * rows * width * columns,
            bytes_accessed=4 * (rows * width + rows * columns) + 3 * width * columns,
            transcendentals=0,
        ),
    )(jnp.stack([bit]).astype(jnp.int32), x, y)


def ffn_kernel(depth, scored, bits, *refs):
    x, c, w_gate, w_up, w_out = refs[:5]
    if scored:
        score, router = refs[5:7]
        rows, d_score, kept, sent = refs[7:11]
    else:
        rows, kept, sent = refs[5:8]
    x_high, x_low, c_high, c_low, xt_high, xt_low, ct_high, ct_low = refs[-8:]
    step = pl.program_id(0)

    @pl.when(step == 0)
    def _():
        for value, high, low, turned_high, turned_low in (
            (x, x_high, x_low, xt_high, xt_low),
            (c, c_high, c_low, ct_high, ct_low),
        ):
            high[...], low[...] = split(value[...])
            turned_high[...], turned_low[...] = split(value[...].T)
        rows[...] = jnp.zeros_like(rows)
        if scored:
            d_score[...] = jnp.zeros_like(d_score)

    gate = dot_nn(x_high[...], w_gate[...]) + dot_nn(x_low[...], w_gate[...])
    up = dot_nn(x_high[...], w_up[...]) + dot_nn(x_low[...], w_up[...])
    cot = dot_nn(c_high[...], w_out[...]) + dot_nn(c_low[...], w_out[...])
    act, slope = gelu_both(gate)
    mix = act * up
    if scored:
        d_score[...] += jnp.sum(cot * mix, axis=1, keepdims=True)
        cot = cot * score[...]
        mix = mix * score[...]
    gate_high, gate_low = split(cot * up * slope)
    up_high, up_low = split(cot * act)
    mix_high, mix_low = split(mix)
    rows[0] += (
        dot_nt(gate_high, w_gate[...])
        + dot_nt(gate_low, w_gate[...])
        + dot_nt(up_high, w_up[...])
        + dot_nt(up_low, w_up[...])
    )
    rows[1] += dot_nt(mix_high, w_out[...]) + dot_nt(mix_low, w_out[...])
    if scored:

        @pl.when(step == pl.num_programs(0) - 1)
        def _():
            into = d_score[...] * score[...] * (1.0 - score[...])
            rows[0] += into * router[...]

    half = xt_high.shape[0] // 2
    for g, (left_high, left_low, high, low) in enumerate(
        (
            (xt_high, xt_low, gate_high, gate_low),
            (xt_high, xt_low, up_high, up_low),
            (ct_high, ct_low, mix_high, mix_low),
        )
    ):
        for mine in (True, False):
            which = bits[0] if mine else 1 - bits[0]
            part = pl.ds(pl.multiple_of(which * half, half), half)
            left = left_high[part, :]
            value = dot_nn(left, high) + dot_nn(left_low[part, :], high) + dot_nn(left, low)
            if mine:
                kept[g] = value
            else:
                sent[g] = packed_blocks([value[n : n + depth] for n in range(0, half, depth)])


def ffn_call(x, c, w_in, w_out, depth, bit, score=None, router=None):
    count, width = x.shape
    units = w_out.shape[1]
    tile, half = 512, width // 2
    tiles = units // tile
    packed = half + power_rows(half // depth)
    scored = score is not None
    whole = pl.BlockSpec((count, width), lambda t, _: (0, 0))
    column = pl.BlockSpec((count, 1), lambda t, _: (0, 0))
    outs = [
        jax.ShapeDtypeStruct((2, count, width), f32),
        jax.ShapeDtypeStruct((count, 1), f32),
        jax.ShapeDtypeStruct((3, half, units), f32),
        jax.ShapeDtypeStruct((3, packed, units), jnp.int16),
    ]
    out_specs = [
        pl.BlockSpec((2, count, width), lambda t, _: (0, 0, 0)),
        column,
        pl.BlockSpec((3, half, tile), lambda t, _: (0, 0, t)),
        pl.BlockSpec((3, packed, tile), lambda t, _: (0, 0, t)),
    ]
    args = [x, c, w_in, w_in, w_out]
    in_specs = [
        whole,
        whole,
        pl.BlockSpec((width, tile), lambda t, _: (0, t)),
        pl.BlockSpec((width, tile), lambda t, _: (0, t + tiles)),
        pl.BlockSpec((width, tile), lambda t, _: (0, t)),
    ]
    if scored:
        args += [score, router]
        in_specs += [column, pl.BlockSpec((1, width), lambda t, _: (0, 0))]
    else:
        outs.pop(1)
        out_specs.pop(1)
    return pl.pallas_call(
        lambda *refs: ffn_kernel(depth, scored, *refs),
        name="ffn",
        grid_spec=pltpu.PrefetchScalarGridSpec(
            num_scalar_prefetch=1,
            grid=(tiles,),
            in_specs=in_specs,
            out_specs=out_specs,
            scratch_shapes=[pltpu.VMEM((count, width), bf16)] * 4
            + [pltpu.VMEM((width, count), bf16)] * 4,
        ),
        out_shape=outs,
        compiler_params=pltpu.CompilerParams(vmem_limit_bytes=56 * 2**20),
        cost_estimate=pl.CostEstimate(
            flops=42 * count * width * units,
            bytes_accessed=24 * count * width + 24 * width * units,
            transcendentals=count * units,
        ),
    )(jnp.stack([bit]).astype(jnp.int32), *args)


def shifted(value, by):
    length = lax.axis_size("seq")
    pairs = [(i, i + by) for i in range(length) if 0 <= i + by < length]
    return unpack_rows(lax.ppermute(pack_rows(value), "seq", pairs))


def product(formula, left_side, right_side):
    return jnp.einsum(
        formula,
        left_side.astype(f32),
        right_side.astype(f32),
        precision=fine,
        preferred_element_type=f32,
    )


def unit_rms(values):
    scale = lax.rsqrt(jnp.mean(values * values, axis=-1, keepdims=True) + eps)
    return values * scale, scale


def norm_back(unit, scale, scaled_grad):
    return scale * (scaled_grad - unit * jnp.mean(scaled_grad * unit, axis=-1, keepdims=True))


def gelu_both(values):
    squared = values * values
    bend = jnp.tanh(GELU_A * (values + GELU_B * squared * values))
    half = 0.5 * (1.0 + bend)
    slope = half + 0.5 * values * (1.0 - bend * bend) * GELU_A * (1.0 + 3.0 * GELU_B * squared)
    return values * half, slope


def local_slots(route_row, row_begin, span_rows, capacity):
    below = jnp.sum((route_row < row_begin).astype(jnp.int32))
    upper = jnp.sum((route_row < row_begin + span_rows).astype(jnp.int32))
    slot = below + jnp.arange(capacity, dtype=jnp.int32)
    index = jnp.arange(route_row.shape[0], dtype=jnp.int32)
    positions = jnp.sum(
        jnp.where(slot[:, None] == index[None, :], route_row[None, :], 0), axis=1
    )
    offsets = positions - row_begin
    matched = (offsets[:, None] == jnp.arange(span_rows, dtype=jnp.int32)[None, :]) & (
        slot < upper
    )[:, None]
    return positions, matched.astype(bf16)


def slot_table(route_row, span_rows, devices, capacity):
    home = route_row // span_rows
    before = jnp.sum((route_row[None, :] < (home * span_rows)[:, None]).astype(jnp.int32), axis=1)
    rank = jnp.arange(route_row.shape[0], dtype=jnp.int32) - before
    place = home * capacity + rank
    return (
        place[:, None] == jnp.arange(devices * capacity, dtype=jnp.int32)[None, :]
    ).astype(bf16)


def split(value):
    high = value.astype(bf16)
    return high, (value - high.astype(f32)).astype(bf16)


def dot_nt(a, b):
    return lax.dot_general(a, b, (((1,), (1,)), ((), ())), preferred_element_type=f32)


def dot_nn(a, b):
    return lax.dot_general(a, b, (((1,), (0,)), ((), ())), preferred_element_type=f32)


def dot_tn(a, b):
    return lax.dot_general(a, b, (((0,), (0,)), ((), ())), preferred_element_type=f32)


def two_heads(value):
    first = lax.broadcasted_iota(jnp.int32, value.shape, 1) < DH
    zero = jnp.zeros_like(value)
    return jnp.concatenate([jnp.where(first, value, zero), jnp.where(first, zero, value)], axis=0)


def one_row_each(value):
    half = value.shape[0] // 2
    first = lax.broadcasted_iota(jnp.int32, (half, value.shape[1]), 1) < DH
    return jnp.where(first, value[:half], value[half:])


def wide_nt(rows_high, rows_low, cols_high, cols_low):
    return dot_nt(
        jnp.concatenate([rows_high, rows_low], axis=1),
        jnp.concatenate([cols_high, cols_high], axis=1),
    ) + dot_nt(rows_high, cols_low)


def wide_nn(a_high, a_low, b_high, b_low):
    columns = b_high.shape[1]
    both = dot_nn(a_high, jnp.concatenate([b_high, b_low], axis=1))
    return both[:, :columns] + both[:, columns:] + dot_nn(a_low, b_high)


def wide_tn(a_high, a_low, b_high, b_low):
    return dot_tn(a_high, b_high) + dot_tn(a_low, b_high) + dot_tn(a_high, b_low)


def pair_probs(query, key_high, key_low, allowed):
    high, low = split(two_heads(query * DH**-0.5))
    scores = wide_nt(key_high, key_low, high, low)
    scores = jnp.where(allowed, scores, -1e30)
    weights = jnp.exp(scores - jnp.max(scores, axis=0, keepdims=True))
    return weights / jnp.sum(weights, axis=0, keepdims=True), high, low


def pair_forward(query, key, value, allowed):
    probs, _, _ = pair_probs(query, *split(key), allowed)
    mixed = wide_tn(*split(value), *split(probs))
    return one_row_each(mixed.T)


def pair_backward(query, key, value, d_out, allowed):
    key_high, key_low = split(key)
    probs, query_high, query_low = pair_probs(query, key_high, key_low, allowed)
    out_high, out_low = split(two_heads(d_out))
    d_value = wide_nn(*split(probs), out_high, out_low)
    d_probs = wide_nt(*split(value), out_high, out_low)
    dots = jnp.sum(probs * d_probs, axis=0, keepdims=True)
    score_high, score_low = split(probs * (d_probs - dots))
    d_key = wide_nn(score_high, score_low, query_high, query_low)
    d_query = wide_tn(key_high, key_low, score_high, score_low)
    return one_row_each(d_query.T) * DH**-0.5, d_key, d_value


def light_allowed(places, seq, block):
    begin, full_len, prefix = places[0], places[1], places[2 + seq]
    shape = (3 * W, 2 * W)
    key_pos = begin + (block - 1) * W + lax.broadcasted_iota(jnp.int32, shape, 0)
    lane = lax.broadcasted_iota(jnp.int32, shape, 1)
    query_pos = begin + block * W + jnp.where(lane < W, lane, lane - W)
    near = jnp.abs(query_pos - key_pos) < W
    inside = (key_pos >= 0) & (key_pos < full_len)
    return near & inside & ((key_pos <= query_pos) | (key_pos < prefix))


def light_forward_kernel(places, q, kv, out):
    seq, block = pl.program_id(0), pl.program_id(1)
    allowed = light_allowed(places, seq, block)
    span = pl.ds(pl.multiple_of(block * W, W), 3 * W)
    for pair in range(HL // 2):
        lanes = slice(2 * DH * pair, 2 * DH * (pair + 1))
        values = slice(IL + 2 * DH * pair, IL + 2 * DH * (pair + 1))
        out[0, :, lanes] = pair_forward(
            q[0, :, lanes], kv[0, span, lanes], kv[0, span, values], allowed
        )


def light_backward_kernel(places, q, kv, d_out, d_q, d_kv):
    seq, block = pl.program_id(0), pl.program_id(1)
    allowed = light_allowed(places, seq, block)
    span = pl.ds(pl.multiple_of(block * W, W), 3 * W)

    @pl.when(block == 0)
    def _():
        d_kv[...] = jnp.zeros_like(d_kv)

    for pair in range(HL // 2):
        lanes = slice(2 * DH * pair, 2 * DH * (pair + 1))
        values = slice(IL + 2 * DH * pair, IL + 2 * DH * (pair + 1))
        d_query, d_key, d_value = pair_backward(
            q[0, :, lanes], kv[0, span, lanes], kv[0, span, values], d_out[0, :, lanes], allowed
        )
        d_q[0, :, lanes] = d_query
        d_kv[0, span, lanes] += d_key
        d_kv[0, span, values] += d_value


def light_call(kernel, places, args, out_shapes, flops):
    seqs, rows, _ = args[0].shape

    def spec(shape):
        if shape[1] == rows:
            return pl.BlockSpec((1, W, shape[2]), lambda s, b, _: (s, b, 0))
        return pl.BlockSpec((1,) + shape[1:], lambda s, b, _: (s, 0, 0))

    return pl.pallas_call(
        kernel,
        name=kernel.__name__,
        grid_spec=pltpu.PrefetchScalarGridSpec(
            num_scalar_prefetch=1,
            grid=(seqs, rows // W),
            in_specs=[spec(a.shape) for a in args],
            out_specs=[spec(o) for o in out_shapes],
        ),
        out_shape=[jax.ShapeDtypeStruct(o, f32) for o in out_shapes],
        compiler_params=pltpu.CompilerParams(vmem_limit_bytes=48 * 2**20),
        cost_estimate=pl.CostEstimate(flops=flops, bytes_accessed=2**23, transcendentals=2**21),
    )(places, *args)


def heavy_allowed(prefix, key_pos, query_pos):
    return (key_pos <= query_pos) | (key_pos < prefix)


def heavy_forward_kernel(places, key_pos, query_pos, q, kv, out):
    allowed = heavy_allowed(places[2 + pl.program_id(0)], key_pos[0], query_pos[0])
    for pair in range(HH // 2):
        lanes = slice(2 * DH * pair, 2 * DH * (pair + 1))
        values = slice(IH + 2 * DH * pair, IH + 2 * DH * (pair + 1))
        out[0, :, lanes] = pair_forward(
            q[0, :, lanes], kv[0, :, lanes], kv[0, :, values], allowed
        )


def heavy_backward_kernel(places, key_pos, query_pos, q, kv, d_out, d_q, d_kv):
    allowed = heavy_allowed(places[2 + pl.program_id(0)], key_pos[0], query_pos[0])
    for pair in range(HH // 2):
        lanes = slice(2 * DH * pair, 2 * DH * (pair + 1))
        values = slice(IH + 2 * DH * pair, IH + 2 * DH * (pair + 1))
        d_query, d_key, d_value = pair_backward(
            q[0, :, lanes], kv[0, :, lanes], kv[0, :, values], d_out[0, :, lanes], allowed
        )
        d_q[0, :, lanes] = d_query
        d_kv[0, :, lanes] = d_key
        d_kv[0, :, values] = d_value


def heavy_call(kernel, places, args, out_shapes, flops):
    def spec(shape):
        return pl.BlockSpec((1,) + shape[1:], lambda s, _: (s, 0, 0))

    return pl.pallas_call(
        kernel,
        name=kernel.__name__,
        grid_spec=pltpu.PrefetchScalarGridSpec(
            num_scalar_prefetch=1,
            grid=(args[0].shape[0],),
            in_specs=[spec(a.shape) for a in args],
            out_specs=[spec(o) for o in out_shapes],
        ),
        out_shape=[jax.ShapeDtypeStruct(o, f32) for o in out_shapes],
        compiler_params=pltpu.CompilerParams(vmem_limit_bytes=48 * 2**20),
        cost_estimate=pl.CostEstimate(flops=flops, bytes_accessed=2**23, transcendentals=2**20),
    )(places, *args)


def on_device(
    tokens,
    cotangent,
    prefix_len,
    query_routes,
    key_routes,
    ffn_routes,
    light_qkv,
    light_out,
    heavy_qkv,
    heavy_out,
    light_ff_in,
    light_ff_out,
    heavy_ff_in,
    heavy_ff_out,
    gains,
    routers,
):
    seqs, rows, width = tokens.shape
    devices = lax.axis_size("seq")
    row_begin = lax.axis_index("seq") * rows
    full_len = rows * devices
    capacity = rows // 4
    units = FH // GROUP

    batch_bits = bit_stages("batch")
    far = devices // GROUP
    device_rows = width // (devices * lax.axis_size("batch"))
    core = lax.axis_index("batch") % 2
    tiled = len(batch_bits) == 1 and device_rows % 8 == 0
    links = Links()

    def joined(*pieces):
        return jnp.concatenate(pieces, axis=1)

    def flat(value):
        return value.reshape(-1, value.shape[-1])

    def chip_gather(value, turned):
        for stage in batch_bits:
            (other,) = links.flip([value], stage)
            value = joined_halves(value, other, own_bit(stage), turned)
            value = value.reshape((value.shape[0] * value.shape[1],) + value.shape[2:])
            turned = False
        return flat(value)

    class Sum:
        def __init__(self, pieces, depth, first, split_already=None):
            self.depth, self.first, self.value, self.groups = depth, first, None, 1
            if not tiled:
                value = joined(
                    *[p if not isinstance(p, tuple) else product("rd,re->de", *p) for p in pieces]
                )
                value = value.reshape((2,) * len(batch_bits) + (-1, value.shape[1]))
                for stage in batch_bits[::-1]:
                    mine = own_bit(stage)
                    sent = lax.dynamic_index_in_dim(value, 1 - mine, 0, keepdims=False)
                    kept = lax.dynamic_index_in_dim(value, mine, 0, keepdims=False)
                    value = kept + links.flip([sent], stage)[0]
                self.value = value.reshape(far, GROUP, device_rows, -1)
                return
            kept, sent = [], []
            if split_already is not None:
                mine, other = split_already
                self.groups = mine.shape[0]
                kept.append(mine.reshape(-1, depth, mine.shape[-1]))
                sent.append(other)
            for p in pieces:
                if isinstance(p, tuple):
                    mine, other = grad_split(*p, core, depth)
                else:
                    p = p.reshape(2, -1, depth, p.shape[1])
                    mine = lax.dynamic_index_in_dim(p, core, 0, keepdims=False)
                    other = lax.dynamic_index_in_dim(p, 1 - core, 0, keepdims=False)
                    power = power_of(other)
                    spare = jnp.zeros((power_rows(len(other)) - len(other), p.shape[3]), f32)
                    other = jnp.concatenate(
                        [flat(steps_of(other, power)), flat(power), spare], axis=0
                    ).astype(jnp.int16)
                kept.append(mine.reshape(-1, depth, mine.shape[-1]))
                sent.append(other)
            got = links.flip(sent, batch_bits[0])
            groups = range(self.groups)
            if first == "near":
                layout = [
                    [((g * far + f) * GROUP + p, 0, depth) for f in range(far) for g in groups]
                    for p in range(GROUP)
                ]
            else:
                layout = [[(g * far + f, 0, depth) for g in groups] for f in range(far)]
            self.sent = send_form(kept, got, layout, first == "far")

        def near(self):
            if not tiled:
                if self.first == "near":
                    self.value = jnp.sum(links.near(jnp.swapaxes(self.value, 0, 1)), axis=0)
                else:
                    self.value = links.near(self.value)
                return
            self.value = links.near(self.sent)
            if self.first == "near":
                groups = self.groups
                layout = [
                    [(f * groups + g, 0, self.depth) for g in range(groups)] for f in range(far)
                ]
                self.sent = arrived(self.value, far * groups, self.depth, layout, True)

        def far(self):
            if not tiled:
                parts = [
                    lax.dynamic_index_in_dim(self.value, far_place() ^ j, 0, keepdims=False)
                    for j in range(far)
                ]
                self.value = sum(links.far(parts))
                return
            self.value = links.far(self.sent)
            if self.first == "far":
                layout = [
                    [
                        (g, p * device_rows, (p + 1) * device_rows)
                        for g in range(self.groups)
                    ]
                    for p in range(GROUP)
                ]
                self.sent = arrived(self.value, self.groups, self.depth, layout)

        def result(self):
            if not tiled:
                return self.value
            groups = self.groups
            if self.first == "near":
                value = arrived(self.value, groups, self.depth)
                return value.reshape(groups, self.depth, -1) if groups > 1 else value
            value = self.value.astype(f32)
            power = value[:, groups * device_rows : groups * (device_rows + 1), None]
            value = value[:, : groups * device_rows]
            return value.reshape(GROUP, groups, device_rows, -1) * jnp.exp2(power - 15.0)

    n_one, r_one = unit_rms(tokens)

    def picker(route_row):
        return local_slots(route_row, row_begin, rows, capacity)

    query_at, query_pick = jax.vmap(picker)(query_routes)
    _, key_pick = jax.vmap(picker)(key_routes)
    _, ffn_pick = jax.vmap(picker)(ffn_routes)
    table = jax.vmap(lambda r: slot_table(r, rows, devices, capacity))(key_routes)

    picked = product("sct,std->scd", jnp.concatenate([query_pick, key_pick], axis=1), n_one)
    query_unit, key_unit_own = picked[:, :capacity], picked[:, capacity:]

    spare = jnp.zeros((gains.shape[0], 128 - 5), bf16)
    before = shifted(tokens[:, rows - W :], 1)
    after_rows = shifted(tokens[:, :W], -1)
    first = links.far_share(joined(light_qkv, heavy_qkv, gains, routers, spare))
    key_far = links.far_share(pack_rows(key_unit_own))
    first = links.near_share(stacked(first, far_place()))
    key_far = stacked(key_far, far_place())
    first, key_far = after([first, key_far], [])

    def unit_parts(value):
        return jnp.swapaxes(value.reshape(value.shape[0], -1, units), 0, 1)

    big = jnp.concatenate(
        [
            unit_parts(heavy_ff_in).reshape(2, GROUP, device_rows, units),
            unit_parts(heavy_ff_out).reshape(1, GROUP, device_rows, units),
        ]
    )
    big = jnp.swapaxes(big, 0, 1).transpose(0, 2, 1, 3).reshape(GROUP, device_rows, 3 * units)
    big = links.near(big)
    first = chip_gather(first, True)
    (first,) = after([first], [big])
    keys = links.near_share(key_far)
    later_far = links.far_share(joined(light_out, heavy_out, light_ff_out, light_ff_in))
    big = links.far_share(big)
    qkv_light, qkv_heavy = first[:, : 3 * IL], first[:, 3 * IL : 3 * IL + 3 * IH]
    small = first[:, 3 * (IL + IH) :].astype(f32)
    gain_one, gain_two = small[:, 0], small[:, 1]
    router_q, router_k, router_f = small[:, 2], small[:, 3], small[:, 4]

    key_slots = unpack_rows(keys.transpose(2, 1, 0, 3, 4)).reshape(seqs, -1, width)
    cot_own = product("sct,std->scd", ffn_pick, cotangent)

    n_ext = unit_rms(jnp.concatenate([before, tokens, after_rows], axis=1))[0]
    normed_ext = n_ext * gain_one
    normed = n_one * gain_one
    light_q = product("std,de->ste", normed, qkv_light[:, :IL])
    light_kv = product("std,de->ste", normed_ext, qkv_light[:, IL:])
    places = jnp.concatenate(
        [jnp.stack([row_begin, jnp.int32(full_len)]), prefix_len]
    ).astype(jnp.int32)
    later = links.near_share(stacked(after(later_far, [light_kv]), far_place()))
    (attended,) = light_call(
        light_forward_kernel, places, (light_q, light_kv), (light_q.shape,), 2**33
    )
    query_rows = query_unit * gain_one
    key_unit = product("skp,spd->skd", table, key_slots)
    key_rows = key_unit * gain_one
    query_score = jax.nn.sigmoid(jnp.sum(query_rows * router_q, axis=-1))
    key_score = jax.nn.sigmoid(jnp.sum(key_rows * router_k, axis=-1))
    heavy_q = product("scd,di->sci", query_rows, qkv_heavy[:, :IH])
    heavy_kv = product("skd,de->ske", key_rows, qkv_heavy[:, IH:])
    heavy_v_raw = heavy_kv[..., IH:]
    heavy_kv = jnp.concatenate(
        [heavy_kv[..., :IH], heavy_v_raw * key_score[..., None]], axis=-1
    )
    key_column = key_routes[:, :, None]
    query_row = jnp.concatenate([query_at, query_at], axis=1)[:, None, :]
    (heavy_mixed,) = heavy_call(
        heavy_forward_kernel,
        places,
        (key_column, query_row, heavy_q, heavy_kv),
        (heavy_q.shape,),
        2**33,
    )
    big = stacked(after(big, [attended]), far_place())
    later = chip_gather(later, True)
    out_light, out_heavy = later[:, :IL], later[:, IL : IL + IH]
    ff_out, ff_in = later[:, IL + IH : IL + IH + FL], later[:, IL + IH + FL :]
    light_branch = product("sti,di->std", attended, out_light)
    big = chip_gather(big, False)
    big_in, big_out = big[:, : 2 * units], big[:, 2 * units :]

    heavy_plain = product("sci,di->scd", heavy_mixed, out_heavy)
    heavy_rows = heavy_plain * query_score[..., None]
    hidden = tokens + light_branch + product("sct,scd->std", query_pick, heavy_rows)

    n_two, r_two = unit_rms(hidden)
    second = n_two * gain_two
    ffn_own = product("sct,std->scd", ffn_pick, second)
    routed = unpack_rows(links.near_share(pack_rows(jnp.stack([ffn_own, cot_own]))))
    ffn_rows, cot_rows = (flat(routed[:, i]) for i in range(2))
    ffn_score = jax.nn.sigmoid(jnp.sum(ffn_rows * router_f, axis=-1, keepdims=True))

    def plain_ffn(x, c, w_in, w_out, score):
        count = w_out.shape[1]
        gate_up = product("rd,de->re", x, w_in)
        act, slope = gelu_both(gate_up[:, :count])
        up = gate_up[:, count:]
        cot = product("rd,df->rf", c, w_out)
        d_score = jnp.sum(cot * act * up, axis=1, keepdims=True)
        mix = act * up * score
        d_in = jnp.concatenate([cot * score * up * slope, cot * score * act], axis=1)
        d_x = product("re,de->rd", d_in, w_in) + d_score * score * (1.0 - score) * router_f
        y = product("rf,df->rd", mix, w_out)
        return jnp.stack([d_x, y]), d_score, [(x, d_in), (c, mix)]

    if tiled:
        light_rows, *grads = ffn_call(
            flat(second), flat(cotangent), ff_in, ff_out, device_rows, core
        )
        d_ff = Sum([], device_rows, "near", grads)
        both, d_score, *grads = ffn_call(
            ffn_rows,
            cot_rows,
            big_in,
            big_out,
            GROUP * device_rows,
            core,
            ffn_score,
            router_f[None],
        )
        d_big_all = Sum([], GROUP * device_rows, "far", grads)
    else:
        light_rows, _, pairs = plain_ffn(flat(second), flat(cotangent), ff_in, ff_out, 1.0)
        d_ff = Sum(pairs, device_rows, "near")
        both, d_score, pairs = plain_ffn(ffn_rows, cot_rows, big_in, big_out, ffn_score)
        d_big_all = Sum(pairs, GROUP * device_rows, "far")
    d_second, light_ff = light_rows.reshape(2, seqs, rows, width)
    d_router_f = jnp.sum(d_score * ffn_score * (1.0 - ffn_score) * ffn_rows, axis=0)
    both = both.reshape(-1, capacity, width)
    layout = [
        [((m * GROUP + p) * seqs + i, 0, capacity) for m in range(2) for i in range(seqs)]
        for p in range(GROUP)
    ]
    back = arrived(
        links.near(send_form([both], [None], layout, False)), 2 * seqs, capacity
    ).reshape(2, seqs, capacity, width)
    ffn_own, out_own = back[0], back[1]
    d_big_all.far()
    d_ff.near()

    output = hidden + light_ff + product("sct,scd->std", ffn_pick, out_own)
    d_second = d_second + product("sct,scd->std", ffn_pick, ffn_own)
    d_gain_two = jnp.sum(d_second * n_two, axis=(0, 1))
    d_hidden = cotangent + norm_back(n_two, r_two, d_second * gain_two)

    d_heavy_rows = product("sct,std->scd", query_pick, d_hidden)
    d_query_score = jnp.sum(d_heavy_rows * heavy_plain, axis=-1)
    d_plain = d_heavy_rows * query_score[..., None]
    d_mixed = product("scd,di->sci", d_plain, out_heavy)
    d_attended = product("std,di->sti", d_hidden, out_light)
    (d_mixed,) = after([d_mixed], list(d_big_all.sent) if tiled else [d_big_all.value])
    d_hq, d_hkv = heavy_call(
        heavy_backward_kernel,
        places,
        (key_column, query_row, heavy_q, heavy_kv, d_mixed),
        (heavy_q.shape, heavy_kv.shape),
        2**34,
    )
    d_hq, d_hkv = after([d_hq, d_hkv], [d_ff.value])
    d_hv = d_hkv[..., IH:]
    d_key_score = jnp.sum(d_hv * heavy_v_raw, axis=-1)
    d_key_in = d_key_score * key_score * (1.0 - key_score)
    d_query_in = d_query_score * query_score * (1.0 - query_score)
    d_kv = jnp.concatenate([d_hkv[..., :IH], d_hv * key_score[..., None]], axis=-1)
    d_key_rows = product("ske,de->skd", d_kv, qkv_heavy[:, IH:]) + d_key_in[..., None] * router_k
    d_query_rows = (
        product("sci,di->scd", d_hq, qkv_heavy[:, :IH]) + d_query_in[..., None] * router_q
    )
    d_router_k = jnp.sum(d_key_in[..., None] * key_rows, axis=(0, 1))
    d_router_q = jnp.sum(d_query_in[..., None] * query_rows, axis=(0, 1))
    d_key_slots = product("skp,skd->spd", table, d_key_rows)
    layout = [
        [((i * far + f) * GROUP + p, 0, capacity) for f in range(far) for i in range(seqs)]
        for p in range(GROUP)
    ]
    key_sent = send_form([d_key_slots.reshape(-1, capacity, width)], [None], layout, False)
    key_near = links.near(key_sent)
    d_ff.far()
    layout = [[(f * seqs + i, 0, capacity) for i in range(seqs)] for f in range(far)]
    d_key_own = links.far(arrived(key_near, far * seqs, capacity, layout, True))
    d_key_own = arrived(d_key_own, seqs, capacity).reshape(seqs, capacity, width)
    d_mid = Sum(
        [
            (flat(d_hidden), flat(attended)),
            (flat(d_plain), flat(heavy_mixed)),
            (flat(query_rows), flat(d_hq)),
            (flat(key_rows), flat(d_kv)),
        ],
        device_rows,
        "near",
    )
    (d_attended,) = after([d_attended], [d_mid.sent if tiled else d_mid.value])

    d_lq, d_lkv = light_call(
        light_backward_kernel,
        places,
        (light_q, light_kv, d_attended),
        (light_q.shape, light_kv.shape),
        2**34,
    )
    d_lq, d_lkv = after([d_lq, d_lkv], [key_near])
    d_ext = product("ste,de->std", d_lkv, qkv_light[:, IL:])
    from_next = shifted(d_ext[:, :W], -1)
    from_prev = shifted(d_ext[:, W + rows :], 1)
    d_own = product("ste,de->std", d_lq, qkv_light[:, :IL]) + product(
        "sct,scd->std", query_pick, d_query_rows
    )
    d_gain_one = (
        jnp.sum(d_ext * n_ext, axis=(0, 1))
        + jnp.sum(d_own * n_one, axis=(0, 1))
        + jnp.sum(d_key_rows * key_unit, axis=(0, 1))
    )
    edges = jnp.pad(from_prev, ((0, 0), (0, rows - W), (0, 0))) + jnp.pad(
        from_next, ((0, 0), (rows - W, 0), (0, 0))
    )
    vectors = jnp.stack([d_gain_one, d_gain_two, d_router_q, d_router_k, d_router_f])
    vectors = jnp.pad(vectors, ((0, 256 - 5), (0, 0))).T
    last = Sum(
        [(flat(normed), flat(d_lq)), (flat(normed_ext), flat(d_lkv)), vectors],
        device_rows,
        "near",
    )
    d_mid.near()
    last.near()
    d_mid.far()
    last.far()
    d_big_all.near()
    d_ff, d_mid, last = d_ff.result(), d_mid.result(), last.result()
    d_big_all = d_big_all.result()
    vectors = last[:, 3 * IL :]

    if tiled:
        big_gate, big_up, d_heavy_ff_out = (
            jnp.swapaxes(d_big_all[:, g], 0, 1).reshape(device_rows, -1) for g in range(3)
        )
        d_heavy_ff_in = joined(big_gate, big_up)
        d_ff_in, d_ff_out = joined(d_ff[0], d_ff[1]), d_ff[2]
    else:
        turned = jnp.swapaxes(d_big_all, 0, 1).reshape(device_rows, GROUP, 3, units)
        big_gate, big_up, d_heavy_ff_out = (
            turned[:, :, g].reshape(device_rows, -1) for g in range(3)
        )
        d_heavy_ff_in = joined(big_gate, big_up)
        d_ff_in, d_ff_out = d_ff[:, : 2 * FL], d_ff[:, 2 * FL :]

    d_normed = (
        d_own
        + d_ext[:, W : W + rows]
        + edges
        + product("sct,scd->std", key_pick, d_key_own)
    )
    grad_tokens = d_hidden + norm_back(n_one, r_one, d_normed * gain_one)

    return (
        output,
        grad_tokens,
        last[:, : 3 * IL],
        d_mid[:, :IL],
        d_mid[:, IL + IH :],
        d_mid[:, IL : IL + IH],
        d_ff_in,
        d_ff_out,
        d_heavy_ff_in,
        d_heavy_ff_out,
        vectors[:, :2],
        vectors[:, 2:5],
    )


def solution(mesh):
    rows = P("batch", "seq", None)
    routes = P("batch", None)
    weight = P(("batch", "seq"), None)
    return jax.shard_map(
        on_device,
        mesh=mesh,
        in_specs=(rows, rows, P("batch"), routes, routes, routes) + (weight,) * 10,
        out_specs=(rows, rows) + (weight,) * 10,
        check_vma=False,
    )
```

```python
import itertools

import jax
import jax.numpy as jnp
from jax import lax
from jax.experimental import pallas as pl
from jax.experimental.pallas import tpu as pltpu
from jax.sharding import PartitionSpec as P

HL = 8
HH = 12
DH = 64
FL = 1024
FH = 4096
W = 128
IL = 512
IH = 768
GROUP = 4

f32 = jnp.float32
bf16 = jnp.bfloat16
fine = lax.Precision.HIGH
eps = 1e-06
GELU_A = 0.7978845608
GELU_B = 0.044715


def bit_stages(axis):
    size, found, step = lax.axis_size(axis), [], 1
    while step < size:
        found.append((axis, step))
        step *= 2
    return found


def own_bit(stage):
    axis, step = stage
    return (lax.axis_index(axis) // step) % 2


def after(values, others):
    values, others = list(values), list(others)
    return list(lax.optimization_barrier(tuple(values) + tuple(others)))[: len(values)]


class Links:
    def __init__(self):
        self.recent = {}

    def queue(self, kind, values):
        recent = self.recent.setdefault(kind, [])
        return after(values, recent[-1]) if recent else values

    def near(self, value):
        groups = [
            list(range(i, i + GROUP)) for i in range(0, lax.axis_size("seq"), GROUP)
        ]
        (value,) = self.queue("near", [value])
        got = lax.all_to_all(value, "seq", 0, 0, axis_index_groups=groups, tiled=True)
        self.recent["near"].append([got])
        return got

    def near_share(self, value):
        return self.near(jnp.broadcast_to(value[None], (GROUP,) + value.shape))

    def far(self, values):
        devices = lax.axis_size("seq")
        sent = self.queue("far", values[1:])
        got = [
            lax.ppermute(v, "seq", [(i, i ^ (GROUP * j)) for i in range(devices)])
            for j, v in enumerate(sent, 1)
        ]
        self.recent["far"].append(got)
        return [values[0]] + got

    def far_share(self, value):
        return self.far([value] * (lax.axis_size("seq") // GROUP))

    def flip(self, values, stage):
        axis, step = stage
        pairs = [(i, i ^ step) for i in range(lax.axis_size(axis))]
        return [lax.ppermute(v, axis, pairs) for v in values]


def far_place():
    return lax.axis_index("seq") // GROUP


def stack_kernel(place, *refs):
    sources, out = refs[:-1], refs[-1]
    for j, source in enumerate(sources):

        @pl.when(pl.program_id(0) == j)
        def _(source=source):
            out[...] = source[...]


def stacked(values, place):
    shape = values[0].shape
    zeros = (0,) * len(shape)
    return pl.pallas_call(
        stack_kernel,
        name="stack",
        grid_spec=pltpu.PrefetchScalarGridSpec(
            num_scalar_prefetch=1,
            grid=(len(values),),
            in_specs=[pl.BlockSpec(shape, lambda j, _: zeros)] * len(values),
            out_specs=pl.BlockSpec((None,) + shape, lambda j, me: (me[0] ^ j,) + zeros),
        ),
        out_shape=jax.ShapeDtypeStruct((len(values),) + shape, values[0].dtype),
        compiler_params=pltpu.CompilerParams(vmem_limit_bytes=40 * 2**20),
        cost_estimate=pl.CostEstimate(
            flops=0, bytes_accessed=4 * values[0].size * len(values), transcendentals=0
        ),
    )(jnp.stack([place]).astype(jnp.int32), *values)


def join_kernel(bit, value, other, out):
    mine = pl.program_id(1) == bit[0]

    @pl.when(mine)
    def _():
        out[...] = value[...]

    @pl.when(jnp.logical_not(mine))
    def _():
        out[...] = other[...]


def joined_halves(value, other, bit, turned):
    steps, inner, rows, width = value.shape
    source = pl.BlockSpec((None, inner, rows, width), lambda i, j, _: (i, 0, 0, 0))
    if turned:
        shape = (2, inner, steps, rows, width)
        target = pl.BlockSpec(
            (None, inner, None, rows, width), lambda i, j, _: (j, 0, i, 0, 0)
        )
    else:
        shape = (2, steps, inner, rows, width)
        target = pl.BlockSpec(
            (None, None, inner, rows, width), lambda i, j, _: (j, i, 0, 0, 0)
        )
    return pl.pallas_call(
        join_kernel,
        name="join",
        grid_spec=pltpu.PrefetchScalarGridSpec(
            num_scalar_prefetch=1,
            grid=(steps, 2),
            in_specs=[source, source],
            out_specs=target,
        ),
        out_shape=jax.ShapeDtypeStruct(shape, value.dtype),
        compiler_params=pltpu.CompilerParams(vmem_limit_bytes=40 * 2**20),
        cost_estimate=pl.CostEstimate(
            flops=0, bytes_accessed=8 * value.size, transcendentals=0
        ),
    )(jnp.stack([bit]).astype(jnp.int32), value, other)


def power_of(block):
    top = jnp.max(jnp.abs(block), axis=-2, keepdims=True)
    return jnp.ceil(jnp.log2(jnp.maximum(top, 1e-30)) + 0.01)


def steps_of(block, power):
    return jnp.floor(block * jnp.exp2(15.0 - power) + 0.5)


def pack_rows(value):
    power = power_of(value)
    extra = jnp.broadcast_to(power, power.shape[:-2] + (8, power.shape[-1]))
    return jnp.concatenate([steps_of(value, power), extra], axis=-2).astype(jnp.int16)


def unpack_rows(packed):
    packed = packed.astype(f32)
    rows = packed.shape[-2] - 8
    return packed[..., :rows, :] * jnp.exp2(packed[..., rows : rows + 1, :] - 15.0)


def power_rows(blocks):
    return -(-blocks // 16) * 16


def packed_blocks(blocks):
    powers = [power_of(block) for block in blocks]
    steps = [steps_of(block, power) for block, power in zip(blocks, powers)]
    powers += [jnp.zeros_like(powers[0])] * (power_rows(len(powers)) - len(powers))
    return jnp.concatenate(steps + powers, axis=0).astype(jnp.int32).astype(jnp.int16)


def block_sum(sources, count, depth):
    totals = [None] * count
    for source in sources:
        steps = source.astype(jnp.int32).astype(f32)
        powers = jnp.exp2(steps[count * depth : count * depth + count] - 15.0)
        for n in range(count):
            block = steps[n * depth : (n + 1) * depth] * powers[n : n + 1]
            totals[n] = block if totals[n] is None else totals[n] + block
    return totals


def give(blocks, layout, place, outs, total):
    if total is None:
        for p, wanted in enumerate(layout):
            outs[0][p] = packed_blocks([blocks[n][low:high] for n, low, high in wanted])
        return
    for p, wanted in enumerate(layout):
        row = 0
        for n, low, high in wanted:
            total[p, row : row + high - low] = blocks[n][low:high]
            row += high - low
    sizes = [high - low for _, low, high in layout[0]]
    for j, out in enumerate(outs):
        rows = total[place ^ j]
        cuts = [sum(sizes[:n]) for n in range(len(sizes) + 1)]
        out[...] = packed_blocks([rows[p:q] for p, q in zip(cuts, cuts[1:])])


def given_form(layout, far, width, tile):
    inner = sum(high - low for _, low, high in layout[0])
    rows = inner + power_rows(len(layout[0]))
    if far:
        return (
            [jax.ShapeDtypeStruct((rows, width), jnp.int16)] * len(layout),
            [pl.BlockSpec((rows, tile), lambda c, _: (0, c))] * len(layout),
            [pltpu.VMEM((len(layout), inner, tile), f32)],
        )
    return (
        [jax.ShapeDtypeStruct((len(layout), rows, width), jnp.int16)],
        [pl.BlockSpec((len(layout), rows, tile), lambda c, _: (0, 0, c))],
        [],
    )


def send_kernel(spans, layout, received, far, place, *refs):
    count = len(spans)
    values, refs = refs[:count], refs[count:]
    others = [None] * count
    if received:
        others, refs = refs[:count], refs[count:]
    outs, total = (refs[:-1], refs[-1]) if far else (refs, None)

    def one(value, other):
        blocks = [value[n] for n in range(value.shape[0])]
        if other is not None:
            parts = [other[...]] if len(other.shape) == 2 else [other[g] for g in range(other.shape[0])]
            each = len(blocks) // len(parts)
            got = [q for part in parts for q in block_sum([part], each, blocks[0].shape[0])]
            blocks = [p + q for p, q in zip(blocks, got)]
        give(blocks, layout, place[0], outs, total)

    for i, (low, high) in enumerate(spans):
        one_piece = lambda i=i: one(values[i], others[i])
        if count == 1:
            one_piece()
        else:
            pl.when((pl.program_id(0) >= low) & (pl.program_id(0) < high))(one_piece)


def send_form(values, others, layout, far):
    widths = [v.shape[2] for v in values]
    tile = max(t for t in (128, 256, 384, 512) if all(w % t == 0 for w in widths))
    spans, begin = [], 0
    for w in widths:
        spans.append((begin, begin + w // tile))
        begin += w // tile
    received = others[0] is not None

    def spec(shape, span):
        lead = (0,) * (len(shape) - 1)
        return pl.BlockSpec(
            shape[:-1] + (tile,),
            lambda c, _: lead + (jnp.clip(c - span[0], 0, span[1] - span[0] - 1),),
        )

    args = list(values) + (list(others) if received else [])
    shapes, out_specs, scratch = given_form(layout, far, sum(widths), tile)
    got = pl.pallas_call(
        lambda *refs: send_kernel(spans, layout, received, far, *refs),
        name="send",
        grid_spec=pltpu.PrefetchScalarGridSpec(
            num_scalar_prefetch=1,
            grid=(begin,),
            in_specs=[spec(v.shape, s) for v, s in zip(args, spans * 2)],
            out_specs=out_specs,
            scratch_shapes=scratch,
        ),
        out_shape=shapes,
        compiler_params=pltpu.CompilerParams(vmem_limit_bytes=48 * 2**20),
        cost_estimate=pl.CostEstimate(
            flops=20 * sum(v.size for v in values),
            bytes_accessed=8 * sum(v.size for v in values),
            transcendentals=0,
        ),
    )(jnp.stack([far_place()]).astype(jnp.int32), *args)
    return got if far else got[0]


def arrived_kernel(sources, count, depth, layout, far, place, *refs):
    if sources is None:
        packed, refs = [refs[0][n] for n in range(refs[0].shape[0])], refs[1:]
    else:
        packed, refs = [r[...] for r in refs[:sources]], refs[sources:]
    blocks = block_sum(packed, count, depth)
    if layout is None:
        for n, block in enumerate(blocks):
            refs[0][n * depth : (n + 1) * depth] = block
        return
    outs, total = (refs[:-1], refs[-1]) if far else (refs, None)
    give(blocks, layout, place[0], outs, total)


def arrived(packed, count, depth, layout=None, far=False):
    args = list(packed) if isinstance(packed, (list, tuple)) else [packed]
    sources = len(args) if isinstance(packed, (list, tuple)) else None
    width = args[0].shape[-1]
    tile = max(t for t in (128, 256, 384, 512) if width % t == 0)
    if layout is None:
        shapes = [jax.ShapeDtypeStruct((count * depth, width), f32)]
        out_specs, scratch = [pl.BlockSpec((count * depth, tile), lambda c, _: (0, c))], []
    else:
        shapes, out_specs, scratch = given_form(layout, far, width, tile)
    lead = (0,) * (args[0].ndim - 1)
    got = pl.pallas_call(
        lambda *refs: arrived_kernel(sources, count, depth, layout, far, *refs),
        name="arrived",
        grid_spec=pltpu.PrefetchScalarGridSpec(
            num_scalar_prefetch=1,
            grid=(width // tile,),
            in_specs=[
                pl.BlockSpec(a.shape[:-1] + (tile,), lambda c, _: lead + (c,)) for a in args
            ],
            out_specs=out_specs,
            scratch_shapes=scratch,
        ),
        out_shape=shapes,
        compiler_params=pltpu.CompilerParams(vmem_limit_bytes=48 * 2**20),
        cost_estimate=pl.CostEstimate(
            flops=10 * sum(a.size for a in args),
            bytes_accessed=4 * sum(a.size for a in args),
            transcendentals=0,
        ),
    )(jnp.stack([far_place()]).astype(jnp.int32), *args)
    return got if far else got[0]


def grad_kernel(depth, bits, x, y, kept, sent, x_high, x_low):
    @pl.when(pl.program_id(0) == 0)
    def _():
        x_high[...], x_low[...] = split(x[...].T)

    y_high, y_low = split(y[...])
    half = x_high.shape[0] // 2

    def part(which):
        rows = pl.ds(pl.multiple_of(which * half, half), half)
        high = x_high[rows, :]
        return dot_nn(high, y_high) + dot_nn(x_low[rows, :], y_high) + dot_nn(high, y_low)

    kept[...] = part(bits[0])
    other = part(1 - bits[0])
    sent[...] = packed_blocks([other[n : n + depth] for n in range(0, half, depth)])


def grad_split(x, y, bit, depth):
    rows, width = x.shape
    half, columns = width // 2, y.shape[1]
    tile = max(t for t in (128, 256, 512) if columns % t == 0)
    packed = half + power_rows(half // depth)
    return pl.pallas_call(
        lambda *refs: grad_kernel(depth, *refs),
        name="grad",
        grid_spec=pltpu.PrefetchScalarGridSpec(
            num_scalar_prefetch=1,
            grid=(columns // tile,),
            in_specs=[
                pl.BlockSpec((rows, width), lambda c, _: (0, 0)),
                pl.BlockSpec((rows, tile), lambda c, _: (0, c)),
            ],
            out_specs=[
                pl.BlockSpec((half, tile), lambda c, _: (0, c)),
                pl.BlockSpec((packed, tile), lambda c, _: (0, c)),
            ],
            scratch_shapes=[pltpu.VMEM((width, rows), bf16)] * 2,
        ),
        out_shape=[
            jax.ShapeDtypeStruct((half, columns), f32),
            jax.ShapeDtypeStruct((packed, columns), jnp.int16),
        ],
        compiler_params=pltpu.CompilerParams(vmem_limit_bytes=48 * 2**20),
        cost_estimate=pl.CostEstimate(
            flops=6 * rows * width * columns,
            bytes_accessed=4 * (rows * width + rows * columns) + 3 * width * columns,
            transcendentals=0,
        ),
    )(jnp.stack([bit]).astype(jnp.int32), x, y)


def ffn_kernel(depth, scored, bits, *refs):
    x, c, w_gate, w_up, w_out = refs[:5]
    if scored:
        score, router = refs[5:7]
        rows, d_score, kept, sent = refs[7:11]
    else:
        rows, kept, sent = refs[5:8]
    x_high, x_low, c_high, c_low, xt_high, xt_low, ct_high, ct_low = refs[-8:]
    step = pl.program_id(0)

    @pl.when(step == 0)
    def _():
        for value, high, low, turned_high, turned_low in (
            (x, x_high, x_low, xt_high, xt_low),
            (c, c_high, c_low, ct_high, ct_low),
        ):
            high[...], low[...] = split(value[...])
            turned_high[...], turned_low[...] = split(value[...].T)
        rows[...] = jnp.zeros_like(rows)
        if scored:
            d_score[...] = jnp.zeros_like(d_score)

    gate = dot_nn(x_high[...], w_gate[...]) + dot_nn(x_low[...], w_gate[...])
    up = dot_nn(x_high[...], w_up[...]) + dot_nn(x_low[...], w_up[...])
    cot = dot_nn(c_high[...], w_out[...]) + dot_nn(c_low[...], w_out[...])
    act, slope = gelu_both(gate)
    mix = act * up
    if scored:
        d_score[...] += jnp.sum(cot * mix, axis=1, keepdims=True)
        cot = cot * score[...]
        mix = mix * score[...]
    gate_high, gate_low = split(cot * up * slope)
    up_high, up_low = split(cot * act)
    mix_high, mix_low = split(mix)
    rows[0] += (
        dot_nt(gate_high, w_gate[...])
        + dot_nt(gate_low, w_gate[...])
        + dot_nt(up_high, w_up[...])
        + dot_nt(up_low, w_up[...])
    )
    rows[1] += dot_nt(mix_high, w_out[...]) + dot_nt(mix_low, w_out[...])
    if scored:

        @pl.when(step == pl.num_programs(0) - 1)
        def _():
            into = d_score[...] * score[...] * (1.0 - score[...])
            rows[0] += into * router[...]

    half = xt_high.shape[0] // 2
    for g, (left_high, left_low, high, low) in enumerate(
        (
            (xt_high, xt_low, gate_high, gate_low),
            (xt_high, xt_low, up_high, up_low),
            (ct_high, ct_low, mix_high, mix_low),
        )
    ):
        for mine in (True, False):
            which = bits[0] if mine else 1 - bits[0]
            part = pl.ds(pl.multiple_of(which * half, half), half)
            left = left_high[part, :]
            value = dot_nn(left, high) + dot_nn(left_low[part, :], high) + dot_nn(left, low)
            if mine:
                kept[g] = value
            else:
                sent[g] = packed_blocks([value[n : n + depth] for n in range(0, half, depth)])


def ffn_call(x, c, w_in, w_out, depth, bit, score=None, router=None):
    count, width = x.shape
    units = w_out.shape[1]
    tile, half = 512, width // 2
    tiles = units // tile
    packed = half + power_rows(half // depth)
    scored = score is not None
    whole = pl.BlockSpec((count, width), lambda t, _: (0, 0))
    column = pl.BlockSpec((count, 1), lambda t, _: (0, 0))
    outs = [
        jax.ShapeDtypeStruct((2, count, width), f32),
        jax.ShapeDtypeStruct((count, 1), f32),
        jax.ShapeDtypeStruct((3, half, units), f32),
        jax.ShapeDtypeStruct((3, packed, units), jnp.int16),
    ]
    out_specs = [
        pl.BlockSpec((2, count, width), lambda t, _: (0, 0, 0)),
        column,
        pl.BlockSpec((3, half, tile), lambda t, _: (0, 0, t)),
        pl.BlockSpec((3, packed, tile), lambda t, _: (0, 0, t)),
    ]
    args = [x, c, w_in, w_in, w_out]
    in_specs = [
        whole,
        whole,
        pl.BlockSpec((width, tile), lambda t, _: (0, t)),
        pl.BlockSpec((width, tile), lambda t, _: (0, t + tiles)),
        pl.BlockSpec((width, tile), lambda t, _: (0, t)),
    ]
    if scored:
        args += [score, router]
        in_specs += [column, pl.BlockSpec((1, width), lambda t, _: (0, 0))]
    else:
        outs.pop(1)
        out_specs.pop(1)
    return pl.pallas_call(
        lambda *refs: ffn_kernel(depth, scored, *refs),
        name="ffn",
        grid_spec=pltpu.PrefetchScalarGridSpec(
            num_scalar_prefetch=1,
            grid=(tiles,),
            in_specs=in_specs,
            out_specs=out_specs,
            scratch_shapes=[pltpu.VMEM((count, width), bf16)] * 4
            + [pltpu.VMEM((width, count), bf16)] * 4,
        ),
        out_shape=outs,
        compiler_params=pltpu.CompilerParams(vmem_limit_bytes=56 * 2**20),
        cost_estimate=pl.CostEstimate(
            flops=42 * count * width * units,
            bytes_accessed=24 * count * width + 24 * width * units,
            transcendentals=count * units,
        ),
    )(jnp.stack([bit]).astype(jnp.int32), *args)


def shifted(value, by):
    length = lax.axis_size("seq")
    pairs = [(i, i + by) for i in range(length) if 0 <= i + by < length]
    return unpack_rows(lax.ppermute(pack_rows(value), "seq", pairs))


def product(formula, left_side, right_side):
    return jnp.einsum(
        formula,
        left_side.astype(f32),
        right_side.astype(f32),
        precision=fine,
        preferred_element_type=f32,
    )


def unit_rms(values):
    scale = lax.rsqrt(jnp.mean(values * values, axis=-1, keepdims=True) + eps)
    return values * scale, scale


def norm_back(unit, scale, scaled_grad):
    return scale * (scaled_grad - unit * jnp.mean(scaled_grad * unit, axis=-1, keepdims=True))


def gelu_both(values):
    squared = values * values
    bend = jnp.tanh(GELU_A * (values + GELU_B * squared * values))
    half = 0.5 * (1.0 + bend)
    slope = half + 0.5 * values * (1.0 - bend * bend) * GELU_A * (1.0 + 3.0 * GELU_B * squared)
    return values * half, slope


def local_slots(route_row, row_begin, span_rows, capacity):
    below = jnp.sum((route_row < row_begin).astype(jnp.int32))
    upper = jnp.sum((route_row < row_begin + span_rows).astype(jnp.int32))
    slot = below + jnp.arange(capacity, dtype=jnp.int32)
    index = jnp.arange(route_row.shape[0], dtype=jnp.int32)
    positions = jnp.sum(
        jnp.where(slot[:, None] == index[None, :], route_row[None, :], 0), axis=1
    )
    offsets = positions - row_begin
    matched = (offsets[:, None] == jnp.arange(span_rows, dtype=jnp.int32)[None, :]) & (
        slot < upper
    )[:, None]
    return positions, matched.astype(bf16)


def slot_table(route_row, span_rows, devices, capacity):
    home = route_row // span_rows
    before = jnp.sum((route_row[None, :] < (home * span_rows)[:, None]).astype(jnp.int32), axis=1)
    rank = jnp.arange(route_row.shape[0], dtype=jnp.int32) - before
    place = home * capacity + rank
    return (
        place[:, None] == jnp.arange(devices * capacity, dtype=jnp.int32)[None, :]
    ).astype(bf16)


def split(value):
    high = value.astype(bf16)
    return high, (value - high.astype(f32)).astype(bf16)


def dot_nt(a, b):
    return lax.dot_general(a, b, (((1,), (1,)), ((), ())), preferred_element_type=f32)


def dot_nn(a, b):
    return lax.dot_general(a, b, (((1,), (0,)), ((), ())), preferred_element_type=f32)


def dot_tn(a, b):
    return lax.dot_general(a, b, (((0,), (0,)), ((), ())), preferred_element_type=f32)


def two_heads(value):
    first = lax.broadcasted_iota(jnp.int32, value.shape, 1) < DH
    zero = jnp.zeros_like(value)
    return jnp.concatenate([jnp.where(first, value, zero), jnp.where(first, zero, value)], axis=0)


def one_row_each(value):
    half = value.shape[0] // 2
    first = lax.broadcasted_iota(jnp.int32, (half, value.shape[1]), 1) < DH
    return jnp.where(first, value[:half], value[half:])


def wide_nt(rows_high, rows_low, cols_high, cols_low):
    return dot_nt(
        jnp.concatenate([rows_high, rows_low], axis=1),
        jnp.concatenate([cols_high, cols_high], axis=1),
    ) + dot_nt(rows_high, cols_low)


def wide_nn(a_high, a_low, b_high, b_low):
    columns = b_high.shape[1]
    both = dot_nn(a_high, jnp.concatenate([b_high, b_low], axis=1))
    return both[:, :columns] + both[:, columns:] + dot_nn(a_low, b_high)


def wide_tn(a_high, a_low, b_high, b_low):
    columns = a_high.shape[1]
    both = dot_tn(jnp.concatenate([a_high, a_low], axis=1), b_high)
    return both[:columns] + both[columns:] + dot_tn(a_high, b_low)


def pair_probs(query, key_high, key_low, allowed):
    high, low = split(two_heads(query * DH**-0.5))
    scores = wide_nt(key_high, key_low, high, low)
    scores = jnp.where(allowed, scores, -1e30)
    weights = jnp.exp(scores - jnp.max(scores, axis=0, keepdims=True))
    return weights * (1.0 / jnp.sum(weights, axis=0, keepdims=True)), high, low


def pair_forward(query, key, value, allowed):
    probs, _, _ = pair_probs(query, *split(key), allowed)
    mixed = wide_tn(*split(value), *split(probs))
    return one_row_each(mixed.T)


def pair_backward(query, key, value, d_out, allowed):
    key_high, key_low = split(key)
    probs, query_high, query_low = pair_probs(query, key_high, key_low, allowed)
    out_high, out_low = split(two_heads(d_out))
    d_value = wide_nn(*split(probs), out_high, out_low)
    d_probs = wide_nt(*split(value), out_high, out_low)
    dots = jnp.sum(probs * d_probs, axis=0, keepdims=True)
    score_high, score_low = split(probs * (d_probs - dots))
    d_key = wide_nn(score_high, score_low, query_high, query_low)
    d_query = wide_tn(key_high, key_low, score_high, score_low)
    return one_row_each(d_query.T) * DH**-0.5, d_key, d_value


def light_allowed(places, seq, block):
    begin, full_len, prefix = places[0], places[1], places[2 + seq]
    shape = (3 * W, W)
    key_pos = begin + (block - 1) * W + lax.broadcasted_iota(jnp.int32, shape, 0)
    query_pos = begin + block * W + lax.broadcasted_iota(jnp.int32, shape, 1)
    near = jnp.abs(query_pos - key_pos) < W
    inside = (key_pos >= 0) & (key_pos < full_len)
    one_head = near & inside & ((key_pos <= query_pos) | (key_pos < prefix))
    one_head = jnp.where(one_head, 1, 0)
    return jnp.concatenate([one_head, one_head], axis=1) > 0


def light_forward_kernel(places, q, kv, out):
    seq, block = pl.program_id(0), pl.program_id(1)
    allowed = light_allowed(places, seq, block)
    span = pl.ds(pl.multiple_of(block * W, W), 3 * W)
    for pair in range(HL // 2):
        lanes = slice(2 * DH * pair, 2 * DH * (pair + 1))
        values = slice(IL + 2 * DH * pair, IL + 2 * DH * (pair + 1))
        out[0, :, lanes] = pair_forward(
            q[0, :, lanes], kv[0, span, lanes], kv[0, span, values], allowed
        )


def light_backward_kernel(places, q, kv, d_out, d_q, d_kv):
    seq, block = pl.program_id(0), pl.program_id(1)
    allowed = light_allowed(places, seq, block)
    span = pl.ds(pl.multiple_of(block * W, W), 3 * W)

    @pl.when(block == 0)
    def _():
        d_kv[...] = jnp.zeros_like(d_kv)

    for pair in range(HL // 2):
        lanes = slice(2 * DH * pair, 2 * DH * (pair + 1))
        values = slice(IL + 2 * DH * pair, IL + 2 * DH * (pair + 1))
        d_query, d_key, d_value = pair_backward(
            q[0, :, lanes], kv[0, span, lanes], kv[0, span, values], d_out[0, :, lanes], allowed
        )
        d_q[0, :, lanes] = d_query
        d_kv[0, span, lanes] += d_key
        d_kv[0, span, values] += d_value


def light_call(kernel, places, args, out_shapes, flops):
    seqs, rows, _ = args[0].shape

    def spec(shape):
        if shape[1] == rows:
            return pl.BlockSpec((1, W, shape[2]), lambda s, b, _: (s, b, 0))
        return pl.BlockSpec((1,) + shape[1:], lambda s, b, _: (s, 0, 0))

    return pl.pallas_call(
        kernel,
        name=kernel.__name__,
        grid_spec=pltpu.PrefetchScalarGridSpec(
            num_scalar_prefetch=1,
            grid=(seqs, rows // W),
            in_specs=[spec(a.shape) for a in args],
            out_specs=[spec(o) for o in out_shapes],
        ),
        out_shape=[jax.ShapeDtypeStruct(o, f32) for o in out_shapes],
        compiler_params=pltpu.CompilerParams(vmem_limit_bytes=48 * 2**20),
        cost_estimate=pl.CostEstimate(flops=flops, bytes_accessed=2**23, transcendentals=2**21),
    )(places, *args)


def heavy_allowed(prefix, key_pos, query_pos):
    return (key_pos <= query_pos) | (key_pos < prefix)


def heavy_forward_kernel(places, key_pos, query_pos, q, kv, out):
    allowed = heavy_allowed(places[2 + pl.program_id(0)], key_pos[0], query_pos[0])
    for pair in range(HH // 2):
        lanes = slice(2 * DH * pair, 2 * DH * (pair + 1))
        values = slice(IH + 2 * DH * pair, IH + 2 * DH * (pair + 1))
        out[0, :, lanes] = pair_forward(
            q[0, :, lanes], kv[0, :, lanes], kv[0, :, values], allowed
        )


def heavy_backward_kernel(places, key_pos, query_pos, q, kv, d_out, d_q, d_kv):
    allowed = heavy_allowed(places[2 + pl.program_id(0)], key_pos[0], query_pos[0])
    for pair in range(HH // 2):
        lanes = slice(2 * DH * pair, 2 * DH * (pair + 1))
        values = slice(IH + 2 * DH * pair, IH + 2 * DH * (pair + 1))
        d_query, d_key, d_value = pair_backward(
            q[0, :, lanes], kv[0, :, lanes], kv[0, :, values], d_out[0, :, lanes], allowed
        )
        d_q[0, :, lanes] = d_query
        d_kv[0, :, lanes] = d_key
        d_kv[0, :, values] = d_value


def heavy_call(kernel, places, args, out_shapes, flops):
    def spec(shape):
        return pl.BlockSpec((1,) + shape[1:], lambda s, _: (s, 0, 0))

    return pl.pallas_call(
        kernel,
        name=kernel.__name__,
        grid_spec=pltpu.PrefetchScalarGridSpec(
            num_scalar_prefetch=1,
            grid=(args[0].shape[0],),
            in_specs=[spec(a.shape) for a in args],
            out_specs=[spec(o) for o in out_shapes],
        ),
        out_shape=[jax.ShapeDtypeStruct(o, f32) for o in out_shapes],
        compiler_params=pltpu.CompilerParams(vmem_limit_bytes=48 * 2**20),
        cost_estimate=pl.CostEstimate(flops=flops, bytes_accessed=2**23, transcendentals=2**20),
    )(places, *args)


def on_device(
    tokens,
    cotangent,
    prefix_len,
    query_routes,
    key_routes,
    ffn_routes,
    light_qkv,
    light_out,
    heavy_qkv,
    heavy_out,
    light_ff_in,
    light_ff_out,
    heavy_ff_in,
    heavy_ff_out,
    gains,
    routers,
):
    seqs, rows, width = tokens.shape
    devices = lax.axis_size("seq")
    row_begin = lax.axis_index("seq") * rows
    full_len = rows * devices
    capacity = rows // 4
    units = FH // GROUP

    batch_bits = bit_stages("batch")
    far = devices // GROUP
    device_rows = width // (devices * lax.axis_size("batch"))
    core = lax.axis_index("batch") % 2
    tiled = len(batch_bits) == 1 and device_rows % 8 == 0
    links = Links()

    def joined(*pieces):
        return jnp.concatenate(pieces, axis=1)

    def flat(value):
        return value.reshape(-1, value.shape[-1])

    def chip_gather(value, turned):
        for stage in batch_bits:
            (other,) = links.flip([value], stage)
            value = joined_halves(value, other, own_bit(stage), turned)
            value = value.reshape((value.shape[0] * value.shape[1],) + value.shape[2:])
            turned = False
        return flat(value)

    class Sum:
        def __init__(self, pieces, depth, first, split_already=None):
            self.depth, self.first, self.value, self.groups = depth, first, None, 1
            if not tiled:
                value = joined(
                    *[p if not isinstance(p, tuple) else product("rd,re->de", *p) for p in pieces]
                )
                value = value.reshape((2,) * len(batch_bits) + (-1, value.shape[1]))
                for stage in batch_bits[::-1]:
                    mine = own_bit(stage)
                    sent = lax.dynamic_index_in_dim(value, 1 - mine, 0, keepdims=False)
                    kept = lax.dynamic_index_in_dim(value, mine, 0, keepdims=False)
                    value = kept + links.flip([sent], stage)[0]
                self.value = value.reshape(far, GROUP, device_rows, -1)
                return
            kept, sent = [], []
            if split_already is not None:
                mine, other = split_already
                self.groups = mine.shape[0]
                kept.append(mine.reshape(-1, depth, mine.shape[-1]))
                sent.append(other)
            for p in pieces:
                if isinstance(p, tuple):
                    mine, other = grad_split(*p, core, depth)
                else:
                    p = p.reshape(2, -1, depth, p.shape[1])
                    mine = lax.dynamic_index_in_dim(p, core, 0, keepdims=False)
                    other = lax.dynamic_index_in_dim(p, 1 - core, 0, keepdims=False)
                    power = power_of(other)
                    spare = jnp.zeros((power_rows(len(other)) - len(other), p.shape[3]), f32)
                    other = jnp.concatenate(
                        [flat(steps_of(other, power)), flat(power), spare], axis=0
                    ).astype(jnp.int16)
                kept.append(mine.reshape(-1, depth, mine.shape[-1]))
                sent.append(other)
            got = links.flip(sent, batch_bits[0])
            groups = range(self.groups)
            if first == "near":
                layout = [
                    [((g * far + f) * GROUP + p, 0, depth) for f in range(far) for g in groups]
                    for p in range(GROUP)
                ]
            else:
                layout = [[(g * far + f, 0, depth) for g in groups] for f in range(far)]
            self.sent = send_form(kept, got, layout, first == "far")

        def near(self):
            if not tiled:
                if self.first == "near":
                    self.value = jnp.sum(links.near(jnp.swapaxes(self.value, 0, 1)), axis=0)
                else:
                    self.value = links.near(self.value)
                return
            self.value = links.near(self.sent)
            if self.first == "near":
                groups = self.groups
                layout = [
                    [(f * groups + g, 0, self.depth) for g in range(groups)] for f in range(far)
                ]
                self.sent = arrived(self.value, far * groups, self.depth, layout, True)

        def far(self):
            if not tiled:
                parts = [
                    lax.dynamic_index_in_dim(self.value, far_place() ^ j, 0, keepdims=False)
                    for j in range(far)
                ]
                self.value = sum(links.far(parts))
                return
            self.value = links.far(self.sent)
            if self.first == "far":
                layout = [
                    [
                        (g, p * device_rows, (p + 1) * device_rows)
                        for g in range(self.groups)
                    ]
                    for p in range(GROUP)
                ]
                self.sent = arrived(self.value, self.groups, self.depth, layout)

        def result(self):
            if not tiled:
                return self.value
            groups = self.groups
            if self.first == "near":
                value = arrived(self.value, groups, self.depth)
                return value.reshape(groups, self.depth, -1) if groups > 1 else value
            value = self.value.astype(f32)
            power = value[:, groups * device_rows : groups * (device_rows + 1), None]
            value = value[:, : groups * device_rows]
            return value.reshape(GROUP, groups, device_rows, -1) * jnp.exp2(power - 15.0)

    n_one, r_one = unit_rms(tokens)

    def picker(route_row):
        return local_slots(route_row, row_begin, rows, capacity)

    query_at, query_pick = jax.vmap(picker)(query_routes)
    _, key_pick = jax.vmap(picker)(key_routes)
    _, ffn_pick = jax.vmap(picker)(ffn_routes)
    table = jax.vmap(lambda r: slot_table(r, rows, devices, capacity))(key_routes)

    picked = product("sct,std->scd", jnp.concatenate([query_pick, key_pick], axis=1), n_one)
    query_unit, key_unit_own = picked[:, :capacity], picked[:, capacity:]

    spare = jnp.zeros((gains.shape[0], 128 - 5), bf16)
    before = shifted(tokens[:, rows - W :], 1)
    after_rows = shifted(tokens[:, :W], -1)
    first = links.far_share(joined(light_qkv, heavy_qkv, gains, routers, spare))
    key_far = links.far_share(pack_rows(key_unit_own))
    first = links.near_share(stacked(first, far_place()))
    key_far = stacked(key_far, far_place())
    first, key_far = after([first, key_far], [])

    def unit_parts(value):
        return jnp.swapaxes(value.reshape(value.shape[0], -1, units), 0, 1)

    big = jnp.concatenate(
        [
            unit_parts(heavy_ff_in).reshape(2, GROUP, device_rows, units),
            unit_parts(heavy_ff_out).reshape(1, GROUP, device_rows, units),
        ]
    )
    big = jnp.swapaxes(big, 0, 1).transpose(0, 2, 1, 3).reshape(GROUP, device_rows, 3 * units)
    big = links.near(big)
    first = chip_gather(first, True)
    (first,) = after([first], [big])
    keys = links.near_share(key_far)
    later_far = links.far_share(joined(light_out, heavy_out, light_ff_out, light_ff_in))
    big = links.far_share(big)
    qkv_light, qkv_heavy = first[:, : 3 * IL], first[:, 3 * IL : 3 * IL + 3 * IH]
    small = first[:, 3 * (IL + IH) :].astype(f32)
    gain_one, gain_two = small[:, 0], small[:, 1]
    router_q, router_k, router_f = small[:, 2], small[:, 3], small[:, 4]

    key_slots = unpack_rows(keys.transpose(2, 1, 0, 3, 4)).reshape(seqs, -1, width)
    cot_own = product("sct,std->scd", ffn_pick, cotangent)

    n_ext = unit_rms(jnp.concatenate([before, tokens, after_rows], axis=1))[0]
    normed_ext = n_ext * gain_one
    normed = n_one * gain_one
    light_q = product("std,de->ste", normed, qkv_light[:, :IL])
    light_kv = product("std,de->ste", normed_ext, qkv_light[:, IL:])
    places = jnp.concatenate(
        [jnp.stack([row_begin, jnp.int32(full_len)]), prefix_len]
    ).astype(jnp.int32)
    later = links.near_share(stacked(after(later_far, [light_kv]), far_place()))
    (attended,) = light_call(
        light_forward_kernel, places, (light_q, light_kv), (light_q.shape,), 2**33
    )
    query_rows = query_unit * gain_one
    key_unit = product("skp,spd->skd", table, key_slots)
    key_rows = key_unit * gain_one
    query_score = jax.nn.sigmoid(jnp.sum(query_rows * router_q, axis=-1))
    key_score = jax.nn.sigmoid(jnp.sum(key_rows * router_k, axis=-1))
    heavy_q = product("scd,di->sci", query_rows, qkv_heavy[:, :IH])
    heavy_kv = product("skd,de->ske", key_rows, qkv_heavy[:, IH:])
    heavy_v_raw = heavy_kv[..., IH:]
    heavy_kv = jnp.concatenate(
        [heavy_kv[..., :IH], heavy_v_raw * key_score[..., None]], axis=-1
    )
    key_column = key_routes[:, :, None]
    query_row = jnp.concatenate([query_at, query_at], axis=1)[:, None, :]
    (heavy_mixed,) = heavy_call(
        heavy_forward_kernel,
        places,
        (key_column, query_row, heavy_q, heavy_kv),
        (heavy_q.shape,),
        2**33,
    )
    big = stacked(after(big, [attended]), far_place())
    later = chip_gather(later, True)
    out_light, out_heavy = later[:, :IL], later[:, IL : IL + IH]
    ff_out, ff_in = later[:, IL + IH : IL + IH + FL], later[:, IL + IH + FL :]
    light_branch = product("sti,di->std", attended, out_light)
    big = chip_gather(big, False)
    big_in, big_out = big[:, : 2 * units], big[:, 2 * units :]

    heavy_plain = product("sci,di->scd", heavy_mixed, out_heavy)
    heavy_rows = heavy_plain * query_score[..., None]
    hidden = tokens + light_branch + product("sct,scd->std", query_pick, heavy_rows)

    n_two, r_two = unit_rms(hidden)
    second = n_two * gain_two
    ffn_own = product("sct,std->scd", ffn_pick, second)
    routed = unpack_rows(links.near_share(pack_rows(jnp.stack([ffn_own, cot_own]))))
    ffn_rows, cot_rows = (flat(routed[:, i]) for i in range(2))
    ffn_score = jax.nn.sigmoid(jnp.sum(ffn_rows * router_f, axis=-1, keepdims=True))

    def plain_ffn(x, c, w_in, w_out, score):
        count = w_out.shape[1]
        gate_up = product("rd,de->re", x, w_in)
        act, slope = gelu_both(gate_up[:, :count])
        up = gate_up[:, count:]
        cot = product("rd,df->rf", c, w_out)
        d_score = jnp.sum(cot * act * up, axis=1, keepdims=True)
        mix = act * up * score
        d_in = jnp.concatenate([cot * score * up * slope, cot * score * act], axis=1)
        d_x = product("re,de->rd", d_in, w_in) + d_score * score * (1.0 - score) * router_f
        y = product("rf,df->rd", mix, w_out)
        return jnp.stack([d_x, y]), d_score, [(x, d_in), (c, mix)]

    if tiled:
        light_rows, *grads = ffn_call(
            flat(second), flat(cotangent), ff_in, ff_out, device_rows, core
        )
        d_ff = Sum([], device_rows, "near", grads)
        both, d_score, *grads = ffn_call(
            ffn_rows,
            cot_rows,
            big_in,
            big_out,
            GROUP * device_rows,
            core,
            ffn_score,
            router_f[None],
        )
        d_big_all = Sum([], GROUP * device_rows, "far", grads)
    else:
        light_rows, _, pairs = plain_ffn(flat(second), flat(cotangent), ff_in, ff_out, 1.0)
        d_ff = Sum(pairs, device_rows, "near")
        both, d_score, pairs = plain_ffn(ffn_rows, cot_rows, big_in, big_out, ffn_score)
        d_big_all = Sum(pairs, GROUP * device_rows, "far")
    d_second, light_ff = light_rows.reshape(2, seqs, rows, width)
    d_router_f = jnp.sum(d_score * ffn_score * (1.0 - ffn_score) * ffn_rows, axis=0)
    both = both.reshape(-1, capacity, width)
    layout = [
        [((m * GROUP + p) * seqs + i, 0, capacity) for m in range(2) for i in range(seqs)]
        for p in range(GROUP)
    ]
    back = arrived(
        links.near(send_form([both], [None], layout, False)), 2 * seqs, capacity
    ).reshape(2, seqs, capacity, width)
    ffn_own, out_own = back[0], back[1]
    d_big_all.far()
    d_ff.near()

    output = hidden + light_ff + product("sct,scd->std", ffn_pick, out_own)
    d_second = d_second + product("sct,scd->std", ffn_pick, ffn_own)
    d_gain_two = jnp.sum(d_second * n_two, axis=(0, 1))
    d_hidden = cotangent + norm_back(n_two, r_two, d_second * gain_two)

    d_heavy_rows = product("sct,std->scd", query_pick, d_hidden)
    d_query_score = jnp.sum(d_heavy_rows * heavy_plain, axis=-1)
    d_plain = d_heavy_rows * query_score[..., None]
    d_mixed = product("scd,di->sci", d_plain, out_heavy)
    d_attended = product("std,di->sti", d_hidden, out_light)
    (d_mixed,) = after([d_mixed], list(d_big_all.sent) if tiled else [d_big_all.value])
    d_hq, d_hkv = heavy_call(
        heavy_backward_kernel,
        places,
        (key_column, query_row, heavy_q, heavy_kv, d_mixed),
        (heavy_q.shape, heavy_kv.shape),
        2**34,
    )
    d_hq, d_hkv = after([d_hq, d_hkv], [d_ff.value])
    d_hv = d_hkv[..., IH:]
    d_key_score = jnp.sum(d_hv * heavy_v_raw, axis=-1)
    d_key_in = d_key_score * key_score * (1.0 - key_score)
    d_query_in = d_query_score * query_score * (1.0 - query_score)
    d_kv = jnp.concatenate([d_hkv[..., :IH], d_hv * key_score[..., None]], axis=-1)
    d_key_rows = product("ske,de->skd", d_kv, qkv_heavy[:, IH:]) + d_key_in[..., None] * router_k
    d_query_rows = (
        product("sci,di->scd", d_hq, qkv_heavy[:, :IH]) + d_query_in[..., None] * router_q
    )
    d_router_k = jnp.sum(d_key_in[..., None] * key_rows, axis=(0, 1))
    d_router_q = jnp.sum(d_query_in[..., None] * query_rows, axis=(0, 1))
    d_key_slots = product("skp,skd->spd", table, d_key_rows)
    layout = [
        [((i * far + f) * GROUP + p, 0, capacity) for f in range(far) for i in range(seqs)]
        for p in range(GROUP)
    ]
    key_sent = send_form([d_key_slots.reshape(-1, capacity, width)], [None], layout, False)
    key_near = links.near(key_sent)
    d_ff.far()
    layout = [[(f * seqs + i, 0, capacity) for i in range(seqs)] for f in range(far)]
    d_key_own = links.far(arrived(key_near, far * seqs, capacity, layout, True))
    d_key_own = arrived(d_key_own, seqs, capacity).reshape(seqs, capacity, width)
    d_mid = Sum(
        [
            (flat(d_hidden), flat(attended)),
            (flat(d_plain), flat(heavy_mixed)),
            (flat(query_rows), flat(d_hq)),
            (flat(key_rows), flat(d_kv)),
        ],
        device_rows,
        "near",
    )
    (d_attended,) = after([d_attended], [d_mid.sent if tiled else d_mid.value])

    d_lq, d_lkv = light_call(
        light_backward_kernel,
        places,
        (light_q, light_kv, d_attended),
        (light_q.shape, light_kv.shape),
        2**34,
    )
    d_lq, d_lkv = after([d_lq, d_lkv], [key_near])
    d_ext = product("ste,de->std", d_lkv, qkv_light[:, IL:])
    from_next = shifted(d_ext[:, :W], -1)
    from_prev = shifted(d_ext[:, W + rows :], 1)
    d_own = product("ste,de->std", d_lq, qkv_light[:, :IL]) + product(
        "sct,scd->std", query_pick, d_query_rows
    )
    d_gain_one = (
        jnp.sum(d_ext * n_ext, axis=(0, 1))
        + jnp.sum(d_own * n_one, axis=(0, 1))
        + jnp.sum(d_key_rows * key_unit, axis=(0, 1))
    )
    edges = jnp.pad(from_prev, ((0, 0), (0, rows - W), (0, 0))) + jnp.pad(
        from_next, ((0, 0), (rows - W, 0), (0, 0))
    )
    vectors = jnp.stack([d_gain_one, d_gain_two, d_router_q, d_router_k, d_router_f])
    vectors = jnp.pad(vectors, ((0, 256 - 5), (0, 0))).T
    last = Sum(
        [(flat(normed), flat(d_lq)), (flat(normed_ext), flat(d_lkv)), vectors],
        device_rows,
        "near",
    )
    d_mid.near()
    last.near()
    d_mid.far()
    last.far()
    d_big_all.near()
    d_ff, d_mid, last = d_ff.result(), d_mid.result(), last.result()
    d_big_all = d_big_all.result()
    vectors = last[:, 3 * IL :]

    if tiled:
        big_gate, big_up, d_heavy_ff_out = (
            jnp.swapaxes(d_big_all[:, g], 0, 1).reshape(device_rows, -1) for g in range(3)
        )
        d_heavy_ff_in = joined(big_gate, big_up)
        d_ff_in, d_ff_out = joined(d_ff[0], d_ff[1]), d_ff[2]
    else:
        turned = jnp.swapaxes(d_big_all, 0, 1).reshape(device_rows, GROUP, 3, units)
        big_gate, big_up, d_heavy_ff_out = (
            turned[:, :, g].reshape(device_rows, -1) for g in range(3)
        )
        d_heavy_ff_in = joined(big_gate, big_up)
        d_ff_in, d_ff_out = d_ff[:, : 2 * FL], d_ff[:, 2 * FL :]

    d_normed = (
        d_own
        + d_ext[:, W : W + rows]
        + edges
        + product("sct,scd->std", key_pick, d_key_own)
    )
    grad_tokens = d_hidden + norm_back(n_one, r_one, d_normed * gain_one)

    return (
        output,
        grad_tokens,
        last[:, : 3 * IL],
        d_mid[:, :IL],
        d_mid[:, IL + IH :],
        d_mid[:, IL : IL + IH],
        d_ff_in,
        d_ff_out,
        d_heavy_ff_in,
        d_heavy_ff_out,
        vectors[:, :2],
        vectors[:, 2:5],
    )


def solution(mesh):
    rows = P("batch", "seq", None)
    routes = P("batch", None)
    weight = P(("batch", "seq"), None)
    return jax.shard_map(
        on_device,
        mesh=mesh,
        in_specs=(rows, rows, P("batch"), routes, routes, routes) + (weight,) * 10,
        out_specs=(rows, rows) + (weight,) * 10,
        check_vma=False,
    )
```
